32 devices in a mesh: dp: 8 (over z, y), tensor: 4 (over x, core).
Axes of the slice: x: 2, y: 2, z: 4, core: 2. Of those that a mesh axis runs over, the one named last changes fastest.
Arguments:
- source: bfloat16 [8, 1024, 512], P('dp', 'tensor'), may hold values from -6 to 6
- target: bfloat16 [8, 1024, 512], P('dp', 'tensor'), may hold values from -6 to 6
- out_grad: bfloat16 [8, 1024, 512], P('dp', 'tensor'), may hold values from -6 to 6
- src_len: int32 [8], P('dp'), may hold values from 1 to 1024, 5120 in all
- tgt_len: int32 [8], P('dp'), may hold values from 1 to 1024, 5120 in all
- owners: int32 [4, 56], P('tensor'), may hold values from 0 to 7, as said below
- master: float32 [4, 64, 64, 512], P('tensor', 'dp'), may hold values from -4 to 4
- rotated_first_moment: float32 [4, 64, 64, 512], P('tensor', 'dp'), may hold values from -40 to 40
- rotated_second_moment: float32 [4, 64, 64, 512], P('tensor', 'dp'), may hold values from 4.096 to 16.384
- stat_left: float32 [4, 64, 64, 64], P('tensor', 'dp'), may hold values from -104857.6 to 461373.44, as said below
- stat_right: float32 [4, 64, 512, 512], P('tensor', 'dp'), may hold values from -13107.2 to 57671.68, as said below
- basis_left: float32 [4, 64, 64, 64], P('tensor', 'dp'), may hold values from -1 to 1, as said below
- basis_right: float32 [4, 64, 512, 512], P('tensor', 'dp'), may hold values from -1 to 1, as said below
- norm_params: float32 [2, 5, 512], replicated, may hold values from -0.3 to 1.4
- norm_one: float32 [2, 5, 512], replicated, may hold values from -40 to 40
- norm_two: float32 [2, 5, 512], replicated, may hold values from 4.096 to 16.384
Outputs:
- decoded: bfloat16 [8, 1024, 512], P('dp', 'tensor')
- src_grad: float32 [8, 1024, 512], P('dp', 'tensor')
- tgt_grad: float32 [8, 1024, 512], P('dp', 'tensor')
- master_new: float32 [4, 64, 64, 512], P('tensor', 'dp')
- moment_one_new: float32 [4, 64, 64, 512], P('tensor', 'dp')
- moment_two_new: float32 [4, 64, 64, 512], P('tensor', 'dp')
- stat_left_new: float32 [4, 64, 64, 64], P('tensor', 'dp')
- stat_right_new: float32 [4, 64, 512, 512], P('tensor', 'dp')
- basis_left_new: float32 [4, 64, 64, 64], P('tensor', 'dp')
- basis_right_new: float32 [4, 64, 512, 512], P('tensor', 'dp')
- copies_new: bfloat16 [4, 64, 64, 512], P('tensor', 'dp')
- norm_new: float32 [2, 5, 512], replicated
- norm_one_new: float32 [2, 5, 512], replicated
- norm_two_new: float32 [2, 5, 512], replicated
The draws below stay inside these ranges and needn't reach their ends.
Inputs may be any that keep to these rules, and one draw needn't show every extreme that they name: `src_len`: the lengths of all 8 sources sum to 5120; some source is 1024 long. `tgt_len`: the lengths of all 8 targets sum to 5120; some target is 1024 long. `owners`: in each tensor index, no owner holds more than 8 blocks, and some owner holds exactly 8. `stat_left`: symmetric positive definite. `stat_right`: symmetric positive definite. `basis_left`: orthogonal to float32 rounding. `basis_right`: orthogonal to float32 rounding.
All inputs are finite; a program needn't handle non-finite values. No bound on the sum of `src_len` or of `tgt_len` on one device may be relied on, other than what follows from the above.
Results may differ from the reference program's by a relative error of at most 0.033.
Values may be sent and summed in bfloat16 or wider, within the bound.
No kernel may reach another device: no remote copies, remote signals or barrier semaphores. Data moves between devices by JAX's collectives and lax.ppermute only.
A program may use at most 192 MiB of HBM per device.

```python
import math
import jax
import jax.numpy as jnp
import numpy as np
from jax import lax

MODEL_WIDTH = 512
HEADS = 8
HEAD_SIZE = 64
PADDED_LENGTH = 1024
STEP = 10
FFB = 32
BLOCKS_DEV = 56
CAP = 8
BLOCK_SLOTS = 64
PAIR_TOTAL = 8
N_DP = 8
N_TENSOR = 4


def owner_table(key):
    slot_count = N_DP * CAP

    def one_row(row_key):
        first_key, second_key, third_key = jax.random.split(row_key, 3)
        chosen = jax.random.randint(first_key, (), 0, N_DP)
        order_rank = jax.random.permutation(second_key, slot_count).astype(jnp.int32)
        slot_ids = jnp.arange(slot_count, dtype=jnp.int32)
        ranking = jnp.where(slot_ids // CAP == chosen, slot_ids - slot_count, order_rank)
        picked = jnp.argsort(ranking)[:BLOCKS_DEV].astype(jnp.int32)
        owner_list = (picked // CAP).astype(jnp.int32)
        shuffle = jax.random.permutation(third_key, BLOCKS_DEV)
        return jnp.zeros((BLOCKS_DEV,), jnp.int32).at[shuffle].set(owner_list)
    return jax.vmap(one_row)(jax.random.split(key, N_TENSOR))


def slot_positions_drawn(owner_row):
    block_ids = jnp.arange(owner_row.shape[0], dtype=jnp.int32)
    same_owner = (owner_row[:, None] == owner_row[None, :]).astype(jnp.int32)
    earlier = (block_ids[None, :] < block_ids[:, None]).astype(jnp.int32)
    rank_of = jnp.sum(same_owner * earlier, axis=1).astype(jnp.int32)
    return (owner_row * CAP + rank_of).astype(jnp.int32)


def block_scales():
    head_count = HEADS // N_TENSOR
    col_count = FFB // N_TENSOR
    block_ids = jnp.arange(BLOCKS_DEV)
    base_scale = MODEL_WIDTH ** (-0.5)
    out_scale = (PADDED_LENGTH / (2.0 * MODEL_WIDTH)) ** 0.5
    is_out = jnp.zeros((BLOCKS_DEV,), jnp.float32)
    for first_id in [3 * head_count, 7 * head_count + 2 * col_count, 11 * head_count + 2 * col_count]:
        is_out = is_out + ((block_ids >= first_id) & (block_ids < first_id + head_count)).astype(jnp.float32)
    is_down = jnp.zeros((BLOCKS_DEV,), jnp.float32)
    for first_id in [4 * head_count + col_count, 12 * head_count + 3 * col_count]:
        is_down = is_down + ((block_ids >= first_id) & (block_ids < first_id + col_count)).astype(jnp.float32)
    return base_scale + is_out * (out_scale - base_scale)


def draw_owners(key, part):
    return owner_table(key)


def draw_master(key, part):
    owner_rows = owner_table(key)
    key = jax.random.fold_in(key, 7)
    slot_row_list = jax.vmap(slot_positions_drawn)(owner_rows)
    match_flags = (slot_row_list[:, None, :] == jnp.arange(BLOCK_SLOTS)[None, :, None]).astype(jnp.float32)
    scales = block_scales()
    used = jnp.sum(match_flags, axis=-1)
    slot_scale = jnp.sum(match_flags * scales[None, None, :], axis=-1) + (1.0 - used) * MODEL_WIDTH ** (-0.5)
    jitter_values = jax.random.truncated_normal(key, -4.0, 4.0, (N_TENSOR, BLOCK_SLOTS, HEAD_SIZE, MODEL_WIDTH), jnp.float32)
    return jitter_values * jnp.minimum(slot_scale, 1.0)[:, :, None, None]


def statistic(key, extent_value, level):
    diagonal_key, jitter_key = jax.random.split(key)
    diagonal_values = jax.random.uniform(diagonal_key, (N_TENSOR, BLOCK_SLOTS, extent_value), jnp.float32)
    diagonal_values = level * jnp.exp(diagonal_values * jnp.log(4.0))
    jitter_values = jax.random.uniform(jitter_key, (N_TENSOR, BLOCK_SLOTS, extent_value, extent_value), jnp.float32, -1.0, 1.0)
    jitter_values = jitter_values * (0.4 * level / extent_value ** 0.5)
    jitter_values = 0.5 * (jitter_values + jnp.swapaxes(jitter_values, -1, -2))
    return jitter_values + diagonal_values[..., None] * jnp.eye(extent_value, dtype=jnp.float32)


def cosine_table(extent_value):
    freq = jnp.arange(extent_value, dtype=jnp.float32)[:, None]
    place = jnp.arange(extent_value, dtype=jnp.float32)[None, :] + 0.5
    table = jnp.cos(jnp.pi * freq * place / extent_value) * (2.0 / extent_value) ** 0.5
    first_row = jnp.where(jnp.arange(extent_value)[:, None] == 0, 0.5 ** 0.5, 1.0)
    return table * first_row


def signed_rotation(one_key, extent_value, table):
    keys = jax.random.split(one_key, 4)
    row_order = jax.random.permutation(keys[0], extent_value)
    col_order = jax.random.permutation(keys[1], extent_value)
    row_sign = 2.0 * jax.random.randint(keys[2], (extent_value,), 0, 2).astype(jnp.float32) - 1.0
    col_sign = 2.0 * jax.random.randint(keys[3], (extent_value,), 0, 2).astype(jnp.float32) - 1.0
    moved = table[row_order][:, col_order]
    return moved * row_sign[:, None] * col_sign[None, :]


def rotation(key, extent_value):
    table = cosine_table(extent_value)
    slot_key_list = jax.random.split(key, N_TENSOR * BLOCK_SLOTS)
    assembled = lax.map(lambda one_key: signed_rotation(one_key, extent_value, table), slot_key_list)
    return assembled.reshape(N_TENSOR, BLOCK_SLOTS, extent_value, extent_value)


def draw_stat_left(key, part):
    key = jax.random.fold_in(key, 11)
    return statistic(key, HEAD_SIZE, 0.025 * MODEL_WIDTH * PAIR_TOTAL * PADDED_LENGTH)


def draw_stat_right(key, part):
    key = jax.random.fold_in(key, 13)
    return statistic(key, MODEL_WIDTH, 0.025 * HEAD_SIZE * PAIR_TOTAL * PADDED_LENGTH)


def draw_basis_left(key, part):
    key = jax.random.fold_in(key, 17)
    return rotation(key, HEAD_SIZE)


def draw_basis_right(key, part):
    key = jax.random.fold_in(key, 19)
    return rotation(key, MODEL_WIDTH)


def draw_norm_params(key, part):
    key = jax.random.fold_in(key, 23)
    gain_key, shift_key = jax.random.split(key)
    gains = jax.random.uniform(gain_key, (5, MODEL_WIDTH), jnp.float32, 0.6, 1.4)
    shifts = jax.random.uniform(shift_key, (5, MODEL_WIDTH), jnp.float32, -0.3, 0.3)
    return jnp.stack([gains, shifts])


def shard_levels(rng, shape, pieces, least, largest):
    gain, own = 1.0, jax.random.fold_in(rng, 6)
    for position, blocks in pieces:
        steps = jnp.exp(jax.random.uniform(jax.random.fold_in(own, position), (blocks,), jnp.float32, least / len(pieces), largest / len(pieces)))
        gain = gain * jnp.repeat(steps, shape[position] // blocks).reshape([-1 if axis == position else 1 for axis in range(len(shape))])
    return gain


def profile(amount, total, reach, slope):
    loads = [(1 << 20) // math.isqrt(grade ** slope) + 1 for grade in range(2, amount + 1)]
    spare, counts = total - reach - (amount - 1), [1] * (amount - 1)
    while spare > 0:
        movable = [i for i in range(amount - 1) if counts[i] < reach]
        mass, left = sum([loads[i] for i in movable]), spare
        for i in movable:
            more = min(reach - counts[i], max(1, left * loads[i] // mass), spare)
            counts[i] = counts[i] + more
            spare = spare - more
    return np.array([reach] + counts)


def uneven_parts(stream_key, number_of, total, most, lean):
    if number_of == 2:
        one = jax.random.randint(stream_key, (), max(1, total - most), min(most, total - 1) + 1)
        return jnp.stack([one, total - one])
    sizes = jnp.asarray(profile(number_of, total, most, lean), jnp.int32)
    pairs = (number_of - 1) // 2
    source_of, sink = sizes[1:1 + 2 * pairs:2], sizes[2:2 + 2 * pairs:2]
    slack = jnp.minimum(source_of - 1, most - sink)
    passed = jax.random.randint(jax.random.fold_in(stream_key, 1), (pairs,), 0, 1 << 20) % (slack + 1)
    sizes = sizes.at[1:1 + 2 * pairs:2].set(source_of - passed).at[2:2 + 2 * pairs:2].set(sink + passed)
    return sizes[jax.random.permutation(jax.random.fold_in(stream_key, 2), number_of)]


def gaussian(rng, dims, scale, most, cuts=(), kind=jnp.bfloat16):
    values = jax.random.normal(rng, dims, jnp.float32) * scale
    if len(cuts) > 0:
        values = shard_levels(rng, dims, cuts, -0.22, 0.18) * values
    return jnp.clip(values, min=-most, max=most).astype(kind)


def setup_inputs(seed: int = 0) -> dict:
    splits = jax.random.split(jax.random.key(seed), 17)
    return {
        "source": gaussian(splits[0], (PAIR_TOTAL, PADDED_LENGTH, MODEL_WIDTH), 1.0, 6.0, ((0, 8), (1, 4))),
        "target": gaussian(splits[1], (PAIR_TOTAL, PADDED_LENGTH, MODEL_WIDTH), 1.0, 6.0, ((0, 8), (1, 4))),
        "out_grad": gaussian(splits[2], (PAIR_TOTAL, PADDED_LENGTH, MODEL_WIDTH), 1.0, 6.0, ((0, 8), (1, 4))),
        "src_len": uneven_parts(splits[3], PAIR_TOTAL, PAIR_TOTAL * PADDED_LENGTH * 5 // 8, PADDED_LENGTH, 1).astype(jnp.int32),
        "tgt_len": uneven_parts(splits[4], PAIR_TOTAL, PAIR_TOTAL * PADDED_LENGTH * 5 // 8, PADDED_LENGTH, 1).astype(jnp.int32),
        "owners": draw_owners(jax.random.fold_in(splits[16], 71), 0),
        "master": draw_master(jax.random.fold_in(splits[16], 71), 0),
        "rotated_first_moment": gaussian(splits[7], (N_TENSOR, BLOCK_SLOTS, HEAD_SIZE, MODEL_WIDTH), (0.1 * (PAIR_TOTAL * PADDED_LENGTH // 2) ** 0.5), 40.0, ((0, 4), (1, 8)), jnp.float32),
        "rotated_second_moment": jnp.clip(jnp.exp(math.log(16.384) - 1.3862944 * jax.random.uniform(splits[8], (N_TENSOR, BLOCK_SLOTS, HEAD_SIZE, MODEL_WIDTH), jnp.float32) ** shard_levels(splits[8], (N_TENSOR, BLOCK_SLOTS, HEAD_SIZE, MODEL_WIDTH), ((0, 4), (1, 8)), -0.2, 0.2)), 4.096, 16.384),
        "stat_left": draw_stat_left(jax.random.fold_in(splits[16], 71), 0),
        "stat_right": draw_stat_right(jax.random.fold_in(splits[16], 71), 0),
        "basis_left": draw_basis_left(jax.random.fold_in(splits[16], 71), 0),
        "basis_right": draw_basis_right(jax.random.fold_in(splits[16], 71), 0),
        "norm_params": draw_norm_params(jax.random.fold_in(splits[16], 71), 0),
        "norm_one": gaussian(splits[14], (2, 5, MODEL_WIDTH), (0.1 * (PAIR_TOTAL * PADDED_LENGTH // 2) ** 0.5), 40.0, (), jnp.float32),
        "norm_two": jnp.clip(jnp.exp(jax.random.uniform(splits[15], (2, 5, MODEL_WIDTH), jnp.float32, math.log(4.096), math.log(16.384))), 4.096, 16.384),
    }


highest = lax.Precision.HIGHEST
rate_matrix = 0.3
rate_vector = 0.6

@jax.custom_vjp
def low(v):
    return lax.optimization_barrier(v.astype(jnp.bfloat16)).astype(jnp.float32)

@jax.custom_vjp
def low_back(v):
    return v

def low_keep(v):
    return (low(v), None)

def low_pass(kept, grad):
    return (grad,)

def back_keep(v):
    return (v, None)

def back_low(kept, grad):
    return (low(grad),)
low.defvjp(low_keep, low_pass)
low_back.defvjp(back_keep, back_low)

def slot_positions(owner_row, capacity):
    block_ids = jnp.arange(owner_row.shape[0], dtype=jnp.int32)
    same_owner = (owner_row[:, None] == owner_row[None, :]).astype(jnp.int32)
    earlier = (block_ids[None, :] < block_ids[:, None]).astype(jnp.int32)
    rank_of = lax.optimization_barrier(jnp.sum(same_owner * earlier, axis=1)).astype(jnp.int32)
    return (owner_row * capacity + rank_of).astype(jnp.int32)

def take_blocks(slot_table, slot_row):
    return slot_table[slot_row]

def place_blocks(gradient_rows, slot_row):
    blank_rows = jnp.zeros((BLOCK_SLOTS,) + gradient_rows.shape[1:], jnp.float32)
    return blank_rows.at[slot_row].set(gradient_rows)

def layer_norm(values, norm_gain, norm_shift):
    center = values - lax.optimization_barrier(jnp.mean(values, axis=-1, keepdims=True))
    spread = lax.optimization_barrier(jnp.mean(center * center, axis=-1, keepdims=True))
    return center * lax.rsqrt(spread + 1e-05) * norm_gain + norm_shift

def project(rows, matrix):
    return jnp.einsum('sd,kd->sk', rows, matrix, precision=highest)

def split_blocks(blocks):
    head_count = HEADS // N_TENSOR
    col_count = FFB // N_TENSOR
    extents = [head_count] * 4 + [col_count] * 2 + [head_count] * 8 + [col_count] * 2
    matrices = []
    offset = 0
    for extent in extents:
        portion = blocks[:, offset:offset + extent]
        matrices.append(portion.reshape(N_TENSOR * extent * HEAD_SIZE, MODEL_WIDTH))
        offset += extent
    return matrices

def attend(query_rows, key_rows, w_query, w_key, w_value, w_out, allowed):
    q_len = query_rows.shape[0]
    k_len = key_rows.shape[0]
    score_scale = HEAD_SIZE ** (-0.5)
    query_v = low(low_back(project(query_rows, w_query))).reshape(q_len, HEADS, HEAD_SIZE)
    key_v = low(low_back(project(key_rows, w_key))).reshape(k_len, HEADS, HEAD_SIZE)
    value_v = low(low_back(project(key_rows, w_value))).reshape(k_len, HEADS, HEAD_SIZE)
    scores = low_back(jnp.einsum('qhe,khe->hqk', query_v, key_v, precision=highest) * score_scale)
    scores = jnp.where(allowed[None], scores, -1e+30)
    top_score = lax.optimization_barrier(jnp.max(scores, axis=-1, keepdims=True))
    powers = jnp.exp(scores - top_score)
    chance = powers / lax.optimization_barrier(jnp.sum(powers, axis=-1, keepdims=True))
    mixed = jnp.einsum('hqk,khe->qhe', low(chance), value_v, precision=highest)
    mixed = low(low_back(mixed)).reshape(q_len, HEADS * HEAD_SIZE)
    return low_back(jnp.einsum('sk,kd->sd', mixed, w_out, precision=highest))

def feed(rows, w_in, w_down):
    hidden = low_back(project(rows, w_in))
    active = low(jax.nn.gelu(hidden, approximate=False))
    return low_back(jnp.einsum('sk,kd->sd', active, w_down, precision=highest))

def pair_forward(blocks, norms, src_vals, tgt_vals, src_size, tgt_size):
    mats = split_blocks(blocks)
    positions = jnp.arange(PADDED_LENGTH, dtype=jnp.int32)
    enc_allowed = jnp.broadcast_to(positions[None, :] < src_size, (PADDED_LENGTH, PADDED_LENGTH))
    dec_allowed = (positions[None, :] <= positions[:, None]) & (positions[None, :] < tgt_size)
    keep_rows = (positions < tgt_size).astype(jnp.float32)[:, None]
    z_one = src_vals + attend(src_vals, src_vals, mats[0], mats[1], mats[2], mats[3], enc_allowed)
    h_one = layer_norm(z_one, norms[0, 0], norms[1, 0])
    z_two = h_one + feed(low(h_one), mats[4], mats[5])
    encoded = layer_norm(z_two, norms[0, 1], norms[1, 1])
    enc_low = low(encoded)
    z_three = tgt_vals + attend(tgt_vals, tgt_vals, mats[6], mats[7], mats[8], mats[9], dec_allowed)
    g_one = layer_norm(z_three, norms[0, 2], norms[1, 2])
    z_four = g_one + attend(low(g_one), enc_low, mats[10], mats[11], mats[12], mats[13], enc_allowed)
    g_two = layer_norm(z_four, norms[0, 3], norms[1, 3])
    z_five = g_two + feed(low(g_two), mats[14], mats[15])
    return layer_norm(z_five, norms[0, 4], norms[1, 4]) * keep_rows

def renew_basis(matrix):
    gram_matrix = jnp.dot(matrix.T, matrix, precision=highest)
    lower_factor = jnp.linalg.cholesky(gram_matrix)
    return jax.scipy.linalg.solve_triangular(lower_factor, matrix.T, lower=True).T

def update_slot(inputs):
    grad_block, weight, first_moment, second_moment, left_stat, right_stat, left_basis, right_basis = inputs
    fix_one = 1.0 - 0.9 ** STEP
    fix_two = 1.0 - 0.999 ** STEP
    turned = jnp.dot(jnp.dot(left_basis.T, grad_block, precision=highest), right_basis, precision=highest)
    first_new = 0.9 * first_moment + 0.1 * turned
    second_new = 0.999 * second_moment + 0.001 * turned * turned
    direction = first_new / fix_one / (jnp.sqrt(second_new / fix_two) + 1e-08)
    update = jnp.dot(jnp.dot(left_basis, direction, precision=highest), right_basis.T, precision=highest)
    weight_new = weight - rate_matrix * (update + 0.01 * weight)
    left_new = 0.95 * left_stat + 0.05 * jnp.dot(grad_block, grad_block.T, precision=highest)
    right_new = 0.95 * right_stat + 0.05 * jnp.dot(grad_block.T, grad_block, precision=highest)
    left_basis_new = renew_basis(jnp.dot(left_new, left_basis, precision=highest))
    right_basis_new = renew_basis(jnp.dot(right_new, right_basis, precision=highest))
    return (weight_new, first_new, second_new, left_new, right_new, left_basis_new, right_basis_new, weight_new.astype(jnp.bfloat16))

def reference(source, target, out_grad, src_len, tgt_len, owners, master, rotated_first_moment, rotated_second_moment, stat_left, stat_right, basis_left, basis_right, norm_params, norm_one, norm_two):
    slot_of = jax.vmap(slot_positions, in_axes=(0, None))(owners, CAP)
    rounded = master.astype(jnp.bfloat16).astype(jnp.float32)
    blocks = jax.vmap(take_blocks)(rounded, slot_of)

    def one_pair(totals, inputs):
        src_row, tgt_row, cot_row, src_size, tgt_size = inputs

        def forward(weights, norms, src_vals, tgt_vals):
            return pair_forward(weights, norms, src_vals, tgt_vals, src_size, tgt_size)
        decoded_row, pullback = jax.vjp(forward, blocks, norm_params, src_row.astype(jnp.float32), tgt_row.astype(jnp.float32))
        grad_blocks, grad_norms, grad_src, grad_tgt = pullback(cot_row.astype(jnp.float32))
        return ((totals[0] + grad_blocks, totals[1] + grad_norms), (decoded_row.astype(jnp.bfloat16), grad_src, grad_tgt))
    start_totals = (jnp.zeros(blocks.shape, jnp.float32), jnp.zeros(norm_params.shape, jnp.float32))
    totals, stacked = lax.scan(one_pair, start_totals, (source, target, out_grad, src_len, tgt_len))
    decoded, src_grad, tgt_grad = stacked
    block_grad, norm_grad = totals
    slot_grad = jax.vmap(place_blocks)(block_grad, slot_of)
    slot_sum_total = N_TENSOR * BLOCK_SLOTS
    flat_inputs = (slot_grad.reshape(slot_sum_total, HEAD_SIZE, MODEL_WIDTH), master.reshape(slot_sum_total, HEAD_SIZE, MODEL_WIDTH), rotated_first_moment.reshape(slot_sum_total, HEAD_SIZE, MODEL_WIDTH), rotated_second_moment.reshape(slot_sum_total, HEAD_SIZE, MODEL_WIDTH), stat_left.reshape(slot_sum_total, HEAD_SIZE, HEAD_SIZE), stat_right.reshape(slot_sum_total, MODEL_WIDTH, MODEL_WIDTH), basis_left.reshape(slot_sum_total, HEAD_SIZE, HEAD_SIZE), basis_right.reshape(slot_sum_total, MODEL_WIDTH, MODEL_WIDTH))
    results = lax.map(update_slot, flat_inputs)
    master_new = results[0].reshape(master.shape)
    moment_one_new = results[1].reshape(master.shape)
    moment_two_new = results[2].reshape(master.shape)
    stat_left_new = results[3].reshape(stat_left.shape)
    stat_right_new = results[4].reshape(stat_right.shape)
    basis_left_new = results[5].reshape(basis_left.shape)
    basis_right_new = results[6].reshape(basis_right.shape)
    copies_new = results[7].reshape(master.shape)
    fix_one = 1.0 - 0.9 ** STEP
    fix_two = 1.0 - 0.999 ** STEP
    norm_one_new = 0.9 * norm_one + 0.1 * norm_grad
    norm_two_new = 0.999 * norm_two + 0.001 * norm_grad * norm_grad
    norm_new = norm_params - rate_vector * (norm_one_new / fix_one) / (jnp.sqrt(norm_two_new / fix_two) + 1e-08)
    return (decoded, src_grad, tgt_grad, master_new, moment_one_new, moment_two_new, stat_left_new, stat_right_new, basis_left_new, basis_right_new, copies_new, norm_new, norm_one_new, norm_two_new)
```

```python
import jax
import jax.numpy as jnp
from jax import lax
from jax.experimental import pallas as pl
from jax.experimental.pallas import tpu as pltpu
from jax.sharding import PartitionSpec as P

HEADS = 8
STEP = 10
FFB = 32


highest = lax.Precision.HIGHEST
rate_matrix = 0.3
rate_vector = 0.6


def slot_positions(owner_row, capacity):
    block_ids = jnp.arange(owner_row.shape[0], dtype=jnp.int32)
    same_owner = (owner_row[:, None] == owner_row[None, :]).astype(jnp.int32)
    earlier = (block_ids[None, :] < block_ids[:, None]).astype(jnp.int32)
    rank_of = jnp.sum(same_owner * earlier, axis=1)
    return owner_row * capacity + rank_of


def layer_norm(values, norm_gain, norm_shift):
    center = values - jnp.mean(values, axis=-1, keepdims=True)
    spread = jnp.mean(center * center, axis=-1, keepdims=True)
    return center * lax.rsqrt(spread + 1e-05) * norm_gain + norm_shift


def project(rows_b, matrix):
    return jnp.einsum("sd,kd->sk", rows_b, matrix, preferred_element_type=jnp.float32)


def gather_rows(rows_b):
    return lax.all_gather(rows_b, "tensor", axis=0, tiled=True)


def scatter_rows(term_fn, row_count):
    return lax.psum_scatter(
        term_fn(jnp.int32(0), row_count * lax.axis_size("tensor")).astype(jnp.bfloat16),
        "tensor",
        scatter_dimension=0,
        tiled=True,
    ).astype(jnp.float32)


def gather_grads(rows_b):
    return lax.all_gather(rows_b, "tensor", axis=0, tiled=True)


def scatter_grads(term_fn, row_count):
    return lax.psum_scatter(
        term_fn(jnp.int32(0), row_count * lax.axis_size("tensor")).astype(jnp.bfloat16),
        "tensor",
        scatter_dimension=0,
        tiled=True,
    ).astype(jnp.float32)


def attention_scores(query_b, key_b, allowed):
    score_scale = query_b.shape[-1] ** (-0.5)
    scores = (
        jnp.einsum("qhe,khe->hqk", query_b, key_b, preferred_element_type=jnp.float32) * score_scale
    )
    return jnp.where(allowed[None], scores, -1e30)


def attention_forward(query_rows, key_rows, weights_four, allowed, head_count, row_count):
    w_query, w_key, w_value, w_out = weights_four
    q_len = query_rows.shape[0]
    k_len = key_rows.shape[0]
    query_b = project(query_rows, w_query).astype(jnp.bfloat16).reshape(q_len, head_count, -1)
    key_b = project(key_rows, w_key).astype(jnp.bfloat16).reshape(k_len, head_count, -1)
    value_b = project(key_rows, w_value).astype(jnp.bfloat16).reshape(k_len, head_count, -1)
    scores = attention_scores(query_b, key_b, allowed)
    top_score = jnp.max(scores, axis=-1, keepdims=True)
    powers = jnp.exp(scores - top_score)
    row_sum = jnp.sum(powers, axis=-1, keepdims=True)
    chance = powers / row_sum
    log_total = top_score + jnp.log(row_sum)
    mixed = jnp.einsum(
        "hqk,khe->qhe", chance.astype(jnp.bfloat16), value_b, preferred_element_type=jnp.float32
    )
    mixed_b = mixed.astype(jnp.bfloat16).reshape(q_len, -1)

    def attention_out_term(row_start, row_total):
        return jnp.dot(mixed_b, w_out, preferred_element_type=jnp.float32)

    branch = scatter_rows(attention_out_term, row_count)
    return (branch, (query_b, key_b, value_b, log_total, mixed_b))


def attention_backward(
    grad_own, saved, weights_four, query_rows, key_rows, allowed, row_count, same_rows
):
    w_query, w_key, w_value, w_out = weights_four
    query_b, key_b, value_b, log_total, mixed_b = saved
    q_len = query_rows.shape[0]
    k_len = key_rows.shape[0]
    grad_full_b = gather_grads(grad_own.astype(jnp.bfloat16))
    grad_mixed_b = jnp.einsum("sd,kd->sk", grad_full_b, w_out, preferred_element_type=jnp.float32)
    grad_mixed_b = grad_mixed_b.astype(jnp.bfloat16).reshape(query_b.shape)
    grad_out_w = jnp.einsum("sk,sd->kd", mixed_b, grad_full_b, preferred_element_type=jnp.float32)
    scores = attention_scores(query_b, key_b, allowed)
    chance = jnp.exp(scores - log_total)
    grad_value = jnp.einsum(
        "hqk,qhe->khe",
        chance.astype(jnp.bfloat16),
        grad_mixed_b,
        preferred_element_type=jnp.float32,
    )
    grad_chance = jnp.einsum(
        "qhe,khe->hqk", grad_mixed_b, value_b, preferred_element_type=jnp.float32
    )
    inner = jnp.sum(chance * grad_chance, axis=-1, keepdims=True)
    grad_score_b = (chance * (grad_chance - inner)).astype(jnp.bfloat16)
    score_scale = query_b.shape[-1] ** (-0.5)
    grad_query = (
        jnp.einsum("hqk,khe->qhe", grad_score_b, key_b, preferred_element_type=jnp.float32)
        * score_scale
    )
    grad_key = (
        jnp.einsum("hqk,qhe->khe", grad_score_b, query_b, preferred_element_type=jnp.float32)
        * score_scale
    )
    grad_query_b = grad_query.astype(jnp.bfloat16).reshape(q_len, -1)
    grad_key_b = grad_key.astype(jnp.bfloat16).reshape(k_len, -1)
    grad_value_b = grad_value.astype(jnp.bfloat16).reshape(k_len, -1)
    grad_weights = [
        jnp.einsum("sk,sd->kd", grad_query_b, query_rows, preferred_element_type=jnp.float32),
        jnp.einsum("sk,sd->kd", grad_key_b, key_rows, preferred_element_type=jnp.float32),
        jnp.einsum("sk,sd->kd", grad_value_b, key_rows, preferred_element_type=jnp.float32),
        grad_out_w,
    ]

    def attention_input_term(row_start, row_total):
        part_query = jnp.dot(grad_query_b, w_query, preferred_element_type=jnp.float32)
        part_key = jnp.dot(grad_key_b, w_key, preferred_element_type=jnp.float32)
        part_key = part_key + jnp.dot(grad_value_b, w_value, preferred_element_type=jnp.float32)
        if same_rows:
            return part_query + part_key
        return jnp.concatenate([part_query, part_key], axis=1)

    return (grad_weights, scatter_grads(attention_input_term, row_count))


def feed_forward(input_rows, w_in, w_down, row_count):
    hidden = project(input_rows, w_in)
    active_b = jax.nn.gelu(hidden, approximate=False).astype(jnp.bfloat16)

    def feed_out_term(row_start, row_total):
        return jnp.dot(active_b, w_down, preferred_element_type=jnp.float32)

    return (scatter_rows(feed_out_term, row_count), (hidden, active_b))


def feed_backward(grad_own, saved, w_in, w_down, input_rows, row_count):
    hidden, active_b = saved
    grad_full_b = gather_grads(grad_own.astype(jnp.bfloat16))
    grad_active = jnp.einsum("sd,kd->sk", grad_full_b, w_down, preferred_element_type=jnp.float32)
    grad_hidden = jax.vjp(lambda inner_value: jax.nn.gelu(inner_value, approximate=False), hidden)[
        1
    ](grad_active)[0]
    grad_hidden_b = grad_hidden.astype(jnp.bfloat16)
    grad_down = jnp.einsum("sk,sd->kd", active_b, grad_full_b, preferred_element_type=jnp.float32)
    grad_in = jnp.einsum("sk,sd->kd", grad_hidden_b, input_rows, preferred_element_type=jnp.float32)

    def feed_input_term(row_start, row_total):
        return jnp.dot(grad_hidden_b, w_in, preferred_element_type=jnp.float32)

    return ([grad_in, grad_down], scatter_grads(feed_input_term, row_count))


F32 = jnp.float32
BF = jnp.bfloat16
NN = (((1,), (0,)), ((), ()))
NT = (((1,), (1,)), ((), ()))
TN = (((0,), (0,)), ((), ()))
FIX_ONE = 1.0 - 0.9**STEP
FIX_TWO = 1.0 - 0.999**STEP


def split(v):
    hi = v.astype(BF)
    return hi, (v - hi.astype(F32)).astype(BF)


def mm(a, b, dims):
    return lax.dot_general(a, b, dims, preferred_element_type=F32)


def mm3(a, b, dims):
    ah, al = a if isinstance(a, tuple) else split(a)
    bh, bl = b if isinstance(b, tuple) else split(b)
    return mm(ah, bh, dims) + (mm(ah, bl, dims) + mm(al, bh, dims))


def before_kernel(s_ref, q_ref, a_ref, m_ref):
    half = s_ref.shape[1] // 2
    q = split(q_ref[0])
    a = 0.95 * mm3(s_ref[0], q, NN)
    a_ref[0] = a
    ah, al = split(a)
    m_ref[0, :half, :] = mm3((ah[:, :half], al[:, :half]), (ah, al), TN)
    m_ref[0, half:, half:] = mm3((ah[:, half:], al[:, half:]), (ah[:, half:], al[:, half:]), TN)


def before(stat, basis):
    n, w, _ = stat.shape
    spec = pl.BlockSpec((1, w, w), lambda i: (i, 0, 0))
    return pl.pallas_call(
        before_kernel,
        grid=(n,),
        in_specs=[spec, spec],
        out_specs=[spec, spec],
        out_shape=[jax.ShapeDtypeStruct(stat.shape, F32)] * 2,
        compiler_params=pltpu.CompilerParams(vmem_limit_bytes=60 << 20),
        cost_estimate=pl.CostEstimate(flops=n * 12 * w**3, bytes_accessed=n * 16 * w * w, transcendentals=0),
        name="before",
    )(stat, basis)


PANEL = 16


def factor_panels(d_ref, count, size):
    rows = lax.broadcasted_iota(jnp.int32, (PANEL, size), 0)
    for p in range(size // PANEL):
        top = p * PANEL
        left = [d_ref[s, top : top + PANEL, 0:size] for s in range(count)]
        right = [d_ref[s, top : top + PANEL, size:] for s in range(count)]
        pivots = [jnp.ones((PANEL, size), F32) for s in range(count)]
        for r in range(PANEL):
            for s in range(count):
                col = jnp.broadcast_to(left[s][:, top + r : top + r + 1], (PANEL, size))
                piv = jnp.broadcast_to(col[r : r + 1, :], (PANEL, size))
                pivots[s] = jnp.where(rows == r, piv, pivots[s])
                if r + 1 < PANEL:
                    fac = jnp.where(rows > r, col * (1.0 / piv), 0.0)
                    left[s] = left[s] - fac * left[s][r : r + 1, :]
                    right[s] = right[s] - fac * right[s][r : r + 1, :]
        for s in range(count):
            scale = lax.rsqrt(pivots[s])
            l_new = left[s] * scale
            r_new = right[s] * scale
            d_ref[s, top : top + PANEL, size:] = r_new
            if top + PANEL < size:
                lh, ll = split(l_new)
                rh, rl = split(r_new)
                lhs = jnp.concatenate([lh, lh, ll], axis=0)
                rhs = jnp.concatenate(
                    [jnp.concatenate([lh, rh], axis=1), jnp.concatenate([ll, rl], axis=1), jnp.concatenate([lh, rh], axis=1)],
                    axis=0,
                )
                d_ref[s, top + PANEL :, :] = d_ref[s, top + PANEL :, :] - mm(lhs[:, top + PANEL :], rhs, TN)


def after_kernel(
    g_ref, w_ref, m1_ref, m2_ref, l_ref, ql_ref, s_ref, q_ref, a_ref, m_ref,
    w_out, m1_out, m2_out, l_out, s_out, qln_out, q_out, c_out,
    gram, gram_left, x_left, diag,
):
    step = pl.program_id(0)
    count = pl.num_programs(0)
    n = q_out.shape[0]
    width = g_ref.shape[2]
    rows = g_ref.shape[1]
    g = g_ref[0]
    q = split(q_ref[0])
    ql = split(ql_ref[0])
    p = mm(g, q[0], NN) + mm(g, q[1], NN)
    turned = mm3(ql, p, TN)
    first = 0.9 * m1_ref[0] + 0.1 * turned
    second = 0.999 * m2_ref[0] + 0.001 * turned * turned
    m1_out[0] = first
    m2_out[0] = second
    direction = first / FIX_ONE / (jnp.sqrt(second / FIX_TWO) + 1e-08)
    update = mm3(ql, mm3(direction, q, NT), NN)
    weight = w_ref[0]
    weight = weight - rate_matrix * (update + 0.01 * weight)
    w_out[0] = weight
    c_out[0] = weight.astype(BF)
    k = mm(g, g, NT)
    left = 0.95 * l_ref[0] + 0.05 * k
    l_out[0] = left
    s_out[0] = 0.95 * s_ref[0] + 0.05 * mm(g, g, TN)
    a = a_ref[0]
    a_parts = split(a)
    b = 0.05 * p
    bh, bl = split(b)
    h = mm(g, a_parts[0], NN) + mm(g, a_parts[1], NN) + 0.5 * mm3(k, (bh, bl), NN)
    q_out[step] = a + mm(jnp.concatenate([g, g], axis=0), jnp.concatenate([bh, bl], axis=0), TN)
    hh, hl = split(h)
    y = jnp.concatenate([hh, bh, hh, bh, hl, bl], axis=0)
    z = jnp.concatenate([bh, hh, bl, hl, bh, hh], axis=0)
    blk = 128
    for i in range(width // blk):
        lo = i * blk
        gram[step, lo : lo + blk, lo:] = m_ref[0, lo : lo + blk, lo:] + mm(y[:, lo : lo + blk], z[:, lo:], TN)
    xl = mm3(left, ql, NN)
    x_left[step] = xl
    gl = mm3(xl, xl, TN)
    gram_left[step] = gl

    @pl.when(step == count - 1)
    def _():
        eye = (lax.broadcasted_iota(jnp.int32, (blk, blk), 0) == lax.broadcasted_iota(jnp.int32, (blk, blk), 1)).astype(F32)
        blocks = width // blk

        def block_step(kk, carry):
            for kb in range(blocks):
                @pl.when(kk == kb)
                def _():
                    for s in range(n):
                        diag[s, :, :blk] = gram[s, kb * blk : kb * blk + blk, kb * blk : kb * blk + blk]
                        diag[s, :, blk:] = eye

            @pl.when(kk == blocks)
            def _():
                for s in range(n):
                    diag[s, :, :blk] = eye
                    diag[s, :rows, :rows] = gram_left[s]
                    diag[s, :, blk:] = eye

            factor_panels(diag, n, blk)

            for kb in range(blocks):
                @pl.when(kk == kb)
                def _():
                    lo = kb * blk
                    hi = lo + blk

                    def one(s, c):
                        inv = diag[s, :, blk:]
                        gram[s, lo:hi, lo:hi] = inv
                        if blocks == 1:
                            return c
                        ih, il = split(inv)
                        lhs = jnp.concatenate([ih, ih, il], axis=1)

                        def scaled(part):
                            ph, plo = split(part)
                            return mm(lhs, jnp.concatenate([ph, plo, ph], axis=0), NN)

                        if kb > 0:
                            gram[s, lo:hi, :lo] = scaled(gram[s, lo:hi, :lo])
                        if hi < width:
                            up = scaled(gram[s, lo:hi, hi:])
                            uh, ul = split(up)
                            rh, rl = split(gram[s, lo:hi, :hi])
                            us = jnp.concatenate([uh, uh, ul], axis=0)
                            vs = jnp.concatenate([uh, ul, uh], axis=0)
                            rs = jnp.concatenate([rh, rl, rh], axis=0)
                            below = mm(us, rs, TN)
                            if kb > 0:
                                gram[s, hi:, :lo] = gram[s, hi:, :lo] - below[:, :lo]
                            gram[s, hi:, lo:hi] = -below[:, lo:]
                            for i in range(kb + 1, blocks):
                                b0 = i * blk
                                gram[s, b0 : b0 + blk, b0:] = gram[s, b0 : b0 + blk, b0:] - mm(
                                    us[:, b0 - hi : b0 - hi + blk], vs[:, b0 - hi :], TN
                                )
                        return c

                    if kb == 0:
                        for s in range(n):
                            for i in range(1, blocks):
                                gram[s, i * blk : i * blk + blk, : i * blk] = jnp.zeros((blk, i * blk), F32)
                    lax.fori_loop(0, n, one, 0)
            return carry

        lax.fori_loop(0, blocks + 1, block_step, 0)

        def finish(s, c):
            x = split(q_out[s])
            for i in range(0, width, 2 * blk):
                hi = i + 2 * blk
                zz = gram[s, i:hi, :hi]
                r_i = lax.broadcasted_iota(jnp.int32, (2 * blk, hi), 0) + i
                c_i = lax.broadcasted_iota(jnp.int32, (2 * blk, hi), 1)
                zz = jnp.where(c_i <= r_i, zz, 0.0)
                q_out[s, :, i:hi] = mm3((x[0][:, :hi], x[1][:, :hi]), zz, NT)
            qln_out[s] = mm3(x_left[s], diag[s, :rows, blk : blk + rows], NT)
            return c

        lax.fori_loop(0, n, finish, 0)


def after(grad, weight, m1, m2, left, ql, stat, q, a, m):
    n, rows, width = weight.shape
    wide = pl.BlockSpec((1, width, width), lambda i: (i, 0, 0))
    flat = pl.BlockSpec((1, rows, width), lambda i: (i, 0, 0))
    small = pl.BlockSpec((1, rows, rows), lambda i: (i, 0, 0))
    sd = jax.ShapeDtypeStruct
    return pl.pallas_call(
        after_kernel,
        grid=(n,),
        in_specs=[flat, flat, flat, flat, small, small, wide, wide, wide, wide],
        out_specs=[
            flat, flat, flat, small, wide,
            pl.BlockSpec((n, rows, rows), lambda i: (0, 0, 0)),
            pl.BlockSpec((n, width, width), lambda i: (0, 0, 0)),
            flat,
        ],
        out_shape=[
            sd(weight.shape, F32), sd(weight.shape, F32), sd(weight.shape, F32), sd(left.shape, F32), sd(stat.shape, F32),
            sd(ql.shape, F32), sd(q.shape, F32), sd(weight.shape, BF),
        ],
        scratch_shapes=[
            pltpu.VMEM((n, width, width), F32),
            pltpu.VMEM((n, rows, rows), F32),
            pltpu.VMEM((n, rows, rows), F32),
            pltpu.VMEM((n, 128, 256), F32),
        ],
        compiler_params=pltpu.CompilerParams(vmem_limit_bytes=62 << 20),
        cost_estimate=pl.CostEstimate(flops=n * 12 * width**3, bytes_accessed=n * 24 * width * width, transcendentals=0),
        name="after",
    )(grad, weight, m1, m2, left, ql, stat, q, a, m)


def per_device(
    source,
    target,
    out_grad,
    src_len,
    tgt_len,
    owners,
    master,
    rotated_first_moment,
    rotated_second_moment,
    stat_left,
    stat_right,
    basis_left,
    basis_right,
    norm_params,
    norm_one,
    norm_two,
):
    tensor_count = lax.axis_size("tensor")
    head_count = HEADS // tensor_count
    col_count = FFB // tensor_count
    capacity = master.shape[1]
    slot_count = capacity * lax.axis_size("dp")
    row_count = source.shape[1]
    seq_full = row_count * tensor_count
    block_rows = master.shape[2]
    width = master.shape[3]
    product, gram = before(stat_right[0], basis_right[0])
    gathered = lax.all_gather(master.astype(jnp.bfloat16), "dp", axis=1, tiled=True)
    slot_of = slot_positions(owners[0], capacity)
    blocks = gathered[0][slot_of]
    extents = [head_count] * 4 + [col_count] * 2 + [head_count] * 8 + [col_count] * 2
    matrices = []
    offset = 0
    for extent in extents:
        matrices.append(blocks[offset : offset + extent].reshape(extent * block_rows, width))
        offset += extent
    positions = lax.iota(jnp.int32, seq_full)
    own_positions = lax.axis_index("tensor") * row_count + lax.iota(jnp.int32, row_count)
    gains = norm_params[0]
    shifts = norm_params[1]

    def pair_step(totals, inputs):
        src_own, tgt_own, cot_own, src_size, tgt_size = inputs
        enc_allowed = jnp.broadcast_to(positions[None, :] < src_size, (seq_full, seq_full))
        dec_allowed = (positions[None, :] <= positions[:, None]) & (positions[None, :] < tgt_size)
        keep_rows = (own_positions < tgt_size).astype(jnp.float32)[:, None]
        src_full = gather_rows(src_own)
        branch_one, saved_one = attention_forward(
            src_full, src_full, matrices[0:4], enc_allowed, head_count, row_count
        )
        z_one = src_own.astype(jnp.float32) + branch_one
        h_one, pull_one = jax.vjp(layer_norm, z_one, gains[0], shifts[0])
        h_one_full = gather_rows(h_one.astype(jnp.bfloat16))
        branch_two, saved_two = feed_forward(h_one_full, matrices[4], matrices[5], row_count)
        z_two = h_one + branch_two
        encoded, pull_two = jax.vjp(layer_norm, z_two, gains[1], shifts[1])
        enc_full = gather_rows(encoded.astype(jnp.bfloat16))
        tgt_full = gather_rows(tgt_own)
        branch_three, saved_three = attention_forward(
            tgt_full, tgt_full, matrices[6:10], dec_allowed, head_count, row_count
        )
        z_three = tgt_own.astype(jnp.float32) + branch_three
        g_one, pull_three = jax.vjp(layer_norm, z_three, gains[2], shifts[2])
        g_one_full = gather_rows(g_one.astype(jnp.bfloat16))
        branch_four, saved_four = attention_forward(
            g_one_full, enc_full, matrices[10:14], enc_allowed, head_count, row_count
        )
        z_four = g_one + branch_four
        g_two, pull_four = jax.vjp(layer_norm, z_four, gains[3], shifts[3])
        g_two_full = gather_rows(g_two.astype(jnp.bfloat16))
        branch_five, saved_five = feed_forward(g_two_full, matrices[14], matrices[15], row_count)
        z_five = g_two + branch_five
        normed, pull_five = jax.vjp(layer_norm, z_five, gains[4], shifts[4])
        decoded_own = (normed * keep_rows).astype(jnp.bfloat16)
        grad_z_five, gain_five, shift_five = pull_five(cot_own.astype(jnp.float32) * keep_rows)
        weights_five, rows_five = feed_backward(
            grad_z_five, saved_five, matrices[14], matrices[15], g_two_full, row_count
        )
        grad_z_four, gain_four, shift_four = pull_four(grad_z_five + rows_five)
        weights_four, rows_four = attention_backward(
            grad_z_four,
            saved_four,
            matrices[10:14],
            g_one_full,
            enc_full,
            enc_allowed,
            row_count,
            False,
        )
        grad_g_one = grad_z_four + rows_four[:, :width]
        grad_encoded = rows_four[:, width:]
        grad_z_three, gain_three, shift_three = pull_three(grad_g_one)
        weights_three, rows_three = attention_backward(
            grad_z_three,
            saved_three,
            matrices[6:10],
            tgt_full,
            tgt_full,
            dec_allowed,
            row_count,
            True,
        )
        tgt_grad_own = grad_z_three + rows_three
        grad_z_two, gain_two, shift_two = pull_two(grad_encoded)
        weights_two, rows_two = feed_backward(
            grad_z_two, saved_two, matrices[4], matrices[5], h_one_full, row_count
        )
        grad_z_one, gain_one, shift_one = pull_one(grad_z_two + rows_two)
        weights_one, rows_one = attention_backward(
            grad_z_one, saved_one, matrices[0:4], src_full, src_full, enc_allowed, row_count, True
        )
        src_grad_own = grad_z_one + rows_one
        grad_list = weights_one + weights_two + weights_three + weights_four + weights_five
        grad_blocks = jnp.concatenate(
            [grad_item.reshape(-1, block_rows, width) for grad_item in grad_list], axis=0
        )
        grad_norms = jnp.stack(
            [
                jnp.stack([gain_one, gain_two, gain_three, gain_four, gain_five]),
                jnp.stack([shift_one, shift_two, shift_three, shift_four, shift_five]),
            ]
        )
        return (
            (totals[0] + grad_blocks, totals[1] + grad_norms),
            (decoded_own, src_grad_own, tgt_grad_own),
        )

    start_totals = (jnp.zeros(blocks.shape, jnp.float32), jnp.zeros(norm_params.shape, jnp.float32))
    totals, stacked = lax.scan(
        pair_step, start_totals, (source, target, out_grad, src_len, tgt_len)
    )
    decoded, src_grad, tgt_grad = stacked
    block_grad, norm_local = totals
    held = slot_of[None, :] == jnp.arange(slot_count, dtype=jnp.int32)[:, None]
    block_of = jnp.sum(jnp.where(held, jnp.arange(slot_of.shape[0], dtype=jnp.int32)[None, :], 0), axis=1)
    used = jnp.any(held, axis=1)
    in_slots = jnp.where(used[:, None, None], block_grad.astype(jnp.bfloat16)[block_of], 0)
    own_grad = lax.psum_scatter(in_slots, "dp", scatter_dimension=0, tiled=True)
    norm_grad = lax.psum(norm_local, ("dp", "tensor"))
    results = after(
        own_grad,
        master[0],
        rotated_first_moment[0],
        rotated_second_moment[0],
        stat_left[0],
        basis_left[0],
        stat_right[0],
        basis_right[0],
        product,
        gram,
    )
    fix_one = 1.0 - 0.9**STEP
    fix_two = 1.0 - 0.999**STEP
    norm_one_new = 0.9 * norm_one + 0.1 * norm_grad
    norm_two_new = 0.999 * norm_two + 0.001 * norm_grad * norm_grad
    norm_new = norm_params - rate_vector * (norm_one_new / fix_one) / (
        jnp.sqrt(norm_two_new / fix_two) + 1e-08
    )
    return (
        decoded,
        src_grad,
        tgt_grad,
        results[0][None],
        results[1][None],
        results[2][None],
        results[3][None],
        results[4][None],
        results[5][None],
        results[6][None],
        results[7][None],
        norm_new,
        norm_one_new,
        norm_two_new,
    )


def solution(mesh):
    in_specs = (
        P("dp", "tensor", None),
        P("dp", "tensor", None),
        P("dp", "tensor", None),
        P("dp"),
        P("dp"),
        P("tensor", None),
        P("tensor", "dp", None, None),
        P("tensor", "dp", None, None),
        P("tensor", "dp", None, None),
        P("tensor", "dp", None, None),
        P("tensor", "dp", None, None),
        P("tensor", "dp", None, None),
        P("tensor", "dp", None, None),
        P(),
        P(),
        P(),
    )
    out_specs = (
        P("dp", "tensor", None),
        P("dp", "tensor", None),
        P("dp", "tensor", None),
        P("tensor", "dp", None, None),
        P("tensor", "dp", None, None),
        P("tensor", "dp", None, None),
        P("tensor", "dp", None, None),
        P("tensor", "dp", None, None),
        P("tensor", "dp", None, None),
        P("tensor", "dp", None, None),
        P("tensor", "dp", None, None),
        P(),
        P(),
        P(),
    )
    return jax.shard_map(
        per_device, mesh=mesh, in_specs=in_specs, out_specs=out_specs, check_vma=False
    )
```

```python
import jax
import jax.numpy as jnp
from jax import lax
from jax.experimental import pallas as pl
from jax.experimental.pallas import tpu as pltpu
from jax.sharding import PartitionSpec as P

HEADS = 8
STEP = 10
FFB = 32


highest = lax.Precision.HIGHEST
rate_matrix = 0.3
rate_vector = 0.6


def slot_positions(owner_row, capacity):
    block_ids = jnp.arange(owner_row.shape[0], dtype=jnp.int32)
    same_owner = (owner_row[:, None] == owner_row[None, :]).astype(jnp.int32)
    earlier = (block_ids[None, :] < block_ids[:, None]).astype(jnp.int32)
    rank_of = jnp.sum(same_owner * earlier, axis=1)
    return owner_row * capacity + rank_of


def layer_norm(values, norm_gain, norm_shift):
    center = values - jnp.mean(values, axis=-1, keepdims=True)
    spread = jnp.mean(center * center, axis=-1, keepdims=True)
    return center * lax.rsqrt(spread + 1e-05) * norm_gain + norm_shift


F32 = jnp.float32
BF = jnp.bfloat16
NN = (((1,), (0,)), ((), ()))
NT = (((1,), (1,)), ((), ()))
TN = (((0,), (0,)), ((), ()))
FIX_ONE = 1.0 - 0.9**STEP
FIX_TWO = 1.0 - 0.999**STEP


def split(v):
    hi = v.astype(BF)
    return hi, (v - hi.astype(F32)).astype(BF)


def mm(a, b, dims):
    return lax.dot_general(a, b, dims, preferred_element_type=F32)


def mm3(a, b, dims):
    ah, al = a if isinstance(a, tuple) else split(a)
    bh, bl = b if isinstance(b, tuple) else split(b)
    return mm(ah, bh, dims) + (mm(ah, bl, dims) + mm(al, bh, dims))


def before_kernel(s_ref, q_ref, a_ref, m_ref):
    half = s_ref.shape[1] // 2
    q = split(q_ref[0])
    a = 0.95 * mm3(s_ref[0], q, NN)
    a_ref[0] = a
    ah, al = split(a)
    m_ref[0, :half, :] = mm3((ah[:, :half], al[:, :half]), (ah, al), TN)
    m_ref[0, half:, half:] = mm3((ah[:, half:], al[:, half:]), (ah[:, half:], al[:, half:]), TN)


def before(stat, basis):
    n, w, _ = stat.shape
    spec = pl.BlockSpec((1, w, w), lambda i: (i, 0, 0))
    return pl.pallas_call(
        before_kernel,
        grid=(n,),
        in_specs=[spec, spec],
        out_specs=[spec, spec],
        out_shape=[jax.ShapeDtypeStruct(stat.shape, F32)] * 2,
        compiler_params=pltpu.CompilerParams(vmem_limit_bytes=60 << 20),
        cost_estimate=pl.CostEstimate(flops=n * 12 * w**3, bytes_accessed=n * 16 * w * w, transcendentals=0),
        name="before",
    )(stat, basis)


PANEL = 16
BLOCK = 128


def reciprocal(v):
    guess = pl.reciprocal(v, approx=True)
    for _ in range(2):
        guess = guess * (2.0 - v * guess)
    return guess


def factor_panels(dm, dw, pm, pw, um, uw, n, panels):
    size = BLOCK
    end = panels * PANEL
    for s in range(n):
        pm[s * PANEL : s * PANEL + PANEL, :] = dm[s * size : s * size + PANEL, :]
        pw[s * PANEL : s * PANEL + PANEL, :] = dw[s * size : s * size + PANEL, :]
    for p in range(panels):
        top = p * PANEL
        low = top + PANEL
        rows = [pm[pl.ds(a, n, stride=PANEL), :] for a in range(PANEL)]
        eyes = [pw[pl.ds(a, n, stride=PANEL), :] for a in range(PANEL)]
        corner = {}
        for a in range(PANEL):
            for b in range(a, PANEL):
                corner[a, b] = jnp.broadcast_to(rows[a][:, top + b : top + b + 1], (n, size))
        for r in range(PANEL):
            inverse = reciprocal(corner[r, r])
            for a in range(r + 1, PANEL):
                factor = corner[r, a] * inverse
                for b in range(a, PANEL):
                    corner[a, b] = corner[a, b] - factor * corner[r, b]
                rows[a] = rows[a] - factor * rows[r]
                eyes[a] = eyes[a] - factor * eyes[r]
            scale = lax.rsqrt(corner[r, r])
            um[pl.ds(r, n, stride=PANEL), :] = rows[r] * scale
            uw[pl.ds(r, n, stride=PANEL), :] = eyes[r] * scale
        pending = []
        for s in range(n):
            base = s * size
            upper = um[s * PANEL : s * PANEL + PANEL, :]
            lower = uw[s * PANEL : s * PANEL + PANEL, :]
            dw[base + top : base + low, :] = lower
            if low < end:
                uh, ul = split(upper)
                lh, ll = split(lower)
                lhs = jnp.concatenate([uh, uh, ul], axis=0)
                high = jnp.concatenate([uh, lh], axis=1)
                rest = jnp.concatenate([ul, ll], axis=1)
                rhs = jnp.concatenate([high, rest, high], axis=0)
                u = mm(lhs[:, low : low + PANEL], rhs, TN)
                pm[s * PANEL : s * PANEL + PANEL, :] = dm[base + low : base + low + PANEL, :] - u[:, :size]
                pw[s * PANEL : s * PANEL + PANEL, :] = dw[base + low : base + low + PANEL, :] - u[:, size:]
                if low + PANEL < end:
                    pending.append((base, lhs, rhs))
        for base, lhs, rhs in pending:
            u = mm(lhs[:, low + PANEL : end], rhs, TN)
            lo, hi = base + low + PANEL, base + end
            dm[lo:hi, :] = dm[lo:hi, :] - u[:, :size]
            dw[lo:hi, :] = dw[lo:hi, :] - u[:, size:]


def after_kernel(
    g_ref, w_ref, m1_ref, m2_ref, l_ref, ql_ref, s_ref, q_ref, a_ref, m_ref,
    w_out, m1_out, m2_out, l_out, s_out, qln_out, q_out, c_out,
    gram, gram_left, x_left, dm, dw, pm, pw, um, uw,
):
    step = pl.program_id(0)
    count = pl.num_programs(0)
    n = q_out.shape[0]
    width = g_ref.shape[2]
    rows = g_ref.shape[1]
    g = g_ref[0]
    q = split(q_ref[0])
    ql = split(ql_ref[0])
    p = mm(g, q[0], NN) + mm(g, q[1], NN)
    turned = mm3(ql, p, TN)
    first = 0.9 * m1_ref[0] + 0.1 * turned
    second = 0.999 * m2_ref[0] + 0.001 * turned * turned
    m1_out[0] = first
    m2_out[0] = second
    direction = first / FIX_ONE / (jnp.sqrt(second / FIX_TWO) + 1e-08)
    update = mm3(ql, mm3(direction, q, NT), NN)
    weight = w_ref[0]
    weight = weight - rate_matrix * (update + 0.01 * weight)
    w_out[0] = weight
    c_out[0] = weight.astype(BF)
    k = mm(g, g, NT)
    left = 0.95 * l_ref[0] + 0.05 * k
    l_out[0] = left
    s_out[0] = 0.95 * s_ref[0] + 0.05 * mm(g, g, TN)
    a = a_ref[0]
    a_parts = split(a)
    b = 0.05 * p
    bh, bl = split(b)
    h = mm(g, a_parts[0], NN) + mm(g, a_parts[1], NN) + 0.5 * mm3(k, (bh, bl), NN)
    q_out[step] = a + mm(jnp.concatenate([g, g], axis=0), jnp.concatenate([bh, bl], axis=0), TN)
    hh, hl = split(h)
    y = jnp.concatenate([hh, bh, hh, bh, hl, bl], axis=0)
    z = jnp.concatenate([bh, hh, bl, hl, bh, hh], axis=0)
    blk = BLOCK
    for i in range(width // blk):
        lo = i * blk
        gram[step, lo : lo + blk, lo:] = m_ref[0, lo : lo + blk, lo:] + mm(y[:, lo : lo + blk], z[:, lo:], TN)
    xl = mm3(left, ql, NN)
    x_left[step] = xl
    gl = mm3(xl, xl, TN)
    gram_left[step] = gl

    @pl.when(step == count - 1)
    def _():
        eye = (lax.broadcasted_iota(jnp.int32, (blk, blk), 0) == lax.broadcasted_iota(jnp.int32, (blk, blk), 1)).astype(F32)
        blocks = width // blk

        def at(s):
            return slice(s * blk, s * blk + blk)

        for s in range(n):
            dm[at(s), :] = eye
            dm[s * blk : s * blk + rows, :rows] = gram_left[s]
            dw[at(s), :] = eye
        factor_panels(dm, dw, pm, pw, um, uw, n, rows // PANEL)
        for s in range(n):
            qln_out[s] = mm3(x_left[s], dw[s * blk : s * blk + rows, :rows], NT)

        def block_step(kk, carry):
            for kb in range(blocks):
                @pl.when(kk == kb)
                def _():
                    for s in range(n):
                        dm[at(s), :] = gram[s, kb * blk : kb * blk + blk, kb * blk : kb * blk + blk]
            for s in range(n):
                dw[at(s), :] = eye
            factor_panels(dm, dw, pm, pw, um, uw, n, blk // PANEL)

            for kb in range(blocks):
                @pl.when(kk == kb)
                def _():
                    lo = kb * blk
                    hi = lo + blk

                    def one(s, c):
                        inv = dw[pl.ds(pl.multiple_of(s * blk, blk), blk), :]
                        gram[s, lo:hi, lo:hi] = inv
                        if blocks == 1:
                            return c
                        ih, il = split(inv)
                        lhs = jnp.concatenate([ih, ih, il], axis=1)

                        def scaled(part):
                            ph, plo = split(part)
                            return mm(lhs, jnp.concatenate([ph, plo, ph], axis=0), NN)

                        if kb > 0:
                            gram[s, lo:hi, :lo] = scaled(gram[s, lo:hi, :lo])
                        if hi < width:
                            up = scaled(gram[s, lo:hi, hi:])
                            uh, ul = split(up)
                            rh, rl = split(gram[s, lo:hi, :hi])
                            us = jnp.concatenate([uh, uh, ul], axis=0)
                            vs = jnp.concatenate([uh, ul, uh], axis=0)
                            rs = jnp.concatenate([rh, rl, rh], axis=0)
                            below = mm(us, rs, TN)
                            if kb > 0:
                                gram[s, hi:, :lo] = gram[s, hi:, :lo] - below[:, :lo]
                            gram[s, hi:, lo:hi] = -below[:, lo:]
                            for i in range(kb + 1, blocks):
                                b0 = i * blk
                                gram[s, b0 : b0 + blk, b0:] = gram[s, b0 : b0 + blk, b0:] - mm(
                                    us[:, b0 - hi : b0 - hi + blk], vs[:, b0 - hi :], TN
                                )
                        return c

                    lax.fori_loop(0, n, one, 0, unroll=min(n, 4))
            return carry

        lax.fori_loop(0, blocks, block_step, 0)

        def finish(s, c):
            x = split(q_out[s])
            for i in range(0, width, 2 * blk):
                hi = i + 2 * blk
                zz = gram[s, i:hi, :hi]
                r_i = lax.broadcasted_iota(jnp.int32, (2 * blk, hi), 0) + i
                c_i = lax.broadcasted_iota(jnp.int32, (2 * blk, hi), 1)
                zz = jnp.where(c_i <= r_i, zz, 0.0)
                q_out[s, :, i:hi] = mm3((x[0][:, :hi], x[1][:, :hi]), zz, NT)
            return c

        lax.fori_loop(0, n, finish, 0, unroll=min(n, 2))


def after(grad, weight, m1, m2, left, ql, stat, q, a, m):
    n, rows, width = weight.shape
    wide = pl.BlockSpec((1, width, width), lambda i: (i, 0, 0))
    flat = pl.BlockSpec((1, rows, width), lambda i: (i, 0, 0))
    small = pl.BlockSpec((1, rows, rows), lambda i: (i, 0, 0))
    sd = jax.ShapeDtypeStruct
    return pl.pallas_call(
        after_kernel,
        grid=(n,),
        in_specs=[flat, flat, flat, flat, small, small, wide, wide, wide, wide],
        out_specs=[
            flat, flat, flat, small, wide,
            pl.BlockSpec((n, rows, rows), lambda i: (0, 0, 0)),
            pl.BlockSpec((n, width, width), lambda i: (0, 0, 0)),
            flat,
        ],
        out_shape=[
            sd(weight.shape, F32), sd(weight.shape, F32), sd(weight.shape, F32), sd(left.shape, F32), sd(stat.shape, F32),
            sd(ql.shape, F32), sd(q.shape, F32), sd(weight.shape, BF),
        ],
        scratch_shapes=[
            pltpu.VMEM((n, width, width), F32),
            pltpu.VMEM((n, rows, rows), F32),
            pltpu.VMEM((n, rows, rows), F32),
            pltpu.VMEM((n * BLOCK, BLOCK), F32),
            pltpu.VMEM((n * BLOCK, BLOCK), F32),
            pltpu.VMEM((n * PANEL, BLOCK), F32),
            pltpu.VMEM((n * PANEL, BLOCK), F32),
            pltpu.VMEM((n * PANEL, BLOCK), F32),
            pltpu.VMEM((n * PANEL, BLOCK), F32),
        ],
        compiler_params=pltpu.CompilerParams(vmem_limit_bytes=62 << 20),
        cost_estimate=pl.CostEstimate(flops=n * 12 * width**3, bytes_accessed=n * 24 * width * width, transcendentals=0),
        name="after",
    )(grad, weight, m1, m2, left, ql, stat, q, a, m)


def swap_core(values):
    count = lax.axis_size("tensor")
    return lax.ppermute(values, "tensor", [(i, i ^ 1) for i in range(count)])


def chip_bits():
    bit, bits = 2, []
    while bit < lax.axis_size("tensor"):
        bits.append(bit)
        bit *= 2
    return bits


def swap_chip(values, bit):
    count = lax.axis_size("tensor")
    return lax.ppermute(values, "tensor", [(i, i ^ bit) for i in range(count)])


def gather_chips(rows):
    for bit in chip_bits():
        other = swap_chip(rows, bit)
        upper = (lax.axis_index("tensor") & bit) != 0
        rows = jnp.where(
            upper, jnp.concatenate([other, rows], axis=0), jnp.concatenate([rows, other], axis=0)
        )
    return rows


def sum_chips(part):
    for bit in chip_bits():
        part = part.astype(BF)
        part = part.astype(F32) + swap_chip(part, bit).astype(F32)
    return part.astype(F32)


def own_rows(values):
    chips = lax.axis_size("tensor") // 2
    count = values.shape[0] // chips
    return lax.dynamic_slice_in_dim(values, (lax.axis_index("tensor") // 2) * count, count, 0)


def sum_chips_own(part):
    for bit in reversed(chip_bits()):
        half = part.shape[0] // 2
        upper = (lax.axis_index("tensor") & bit) != 0
        keep = jnp.where(upper, part[half:], part[:half])
        give = jnp.where(upper, part[:half], part[half:]).astype(BF)
        part = keep.astype(F32) + swap_chip(give, bit).astype(F32)
    return part


def sum_everywhere(values):
    values = values + swap_core(values)
    count = lax.axis_size("dp")
    if count & (count - 1):
        return lax.psum(values, "dp")
    bit = 1
    while bit < count:
        values = values + lax.ppermute(values, "dp", [(i, i ^ bit) for i in range(count)])
        bit *= 2
    return values


def project(rows, matrix):
    return mm(rows, matrix, NT)


def join_core(own, width):
    other = swap_core(own)
    half = width // 2
    parts = []
    for start in range(0, own.shape[1], width):
        parts.append(other[:, start + half : start + width])
        parts.append(other[:, start : start + half])
    return jnp.concatenate([own, jnp.concatenate(parts, axis=1)], axis=0)


def attention_scores(query, key, allowed):
    scale = query.shape[-1] ** (-0.5)
    scores = jnp.einsum("qhe,khe->hqk", query, key, preferred_element_type=F32) * scale
    return jnp.where(allowed[None], scores, -1e30)


def heads_of(rows, size):
    return rows.reshape(rows.shape[0], -1, size)


def attention_forward(query_rows, key_rows, weights, allowed, size):
    w_query, w_key, w_value, w_out = weights
    width = w_query.shape[0]
    query = project(query_rows, w_query).astype(BF)
    pair = project(key_rows, jnp.concatenate([w_key, w_value], axis=0)).astype(BF)
    pair = join_core(pair, width)
    key, value = pair[:, :width], pair[:, width:]
    scores = attention_scores(heads_of(query, size), heads_of(key, size), allowed)
    top = jnp.max(scores, axis=-1, keepdims=True)
    powers = jnp.exp(scores - top)
    total = jnp.sum(powers, axis=-1, keepdims=True)
    chance = powers / total
    log_total = top + jnp.log(total)
    mixed = jnp.einsum("hqk,khe->qhe", chance.astype(BF), heads_of(value, size), preferred_element_type=F32)
    mixed = mixed.astype(BF).reshape(query.shape)
    return mm(mixed, w_out, NN), (query, key, value, log_total, mixed)


def attention_backward(grad, saved, weights, query_rows, key_rows, allowed, size):
    w_query, w_key, w_value, w_out = weights
    query, key, value, log_total, mixed = saved
    width = query.shape[1]
    own = key_rows.shape[0]
    grad_b = grad.astype(BF)
    grad_mixed = heads_of(mm(grad_b, w_out, NT).astype(BF), size)
    grad_out_w = mm(mixed, grad_b, TN)
    query_h, key_h, value_h = heads_of(query, size), heads_of(key, size), heads_of(value, size)
    scores = attention_scores(query_h, key_h, allowed)
    chance = jnp.exp(scores - log_total)
    grad_value = jnp.einsum("hqk,qhe->khe", chance.astype(BF), grad_mixed, preferred_element_type=F32)
    grad_chance = jnp.einsum("qhe,khe->hqk", grad_mixed, value_h, preferred_element_type=F32)
    inner = jnp.sum(chance * grad_chance, axis=-1, keepdims=True)
    grad_score = (chance * (grad_chance - inner)).astype(BF)
    scale = size ** (-0.5)
    grad_query = jnp.einsum("hqk,khe->qhe", grad_score, key_h, preferred_element_type=F32) * scale
    grad_key = jnp.einsum("hqk,qhe->khe", grad_score, query_h, preferred_element_type=F32) * scale
    grad_query = grad_query.astype(BF).reshape(query.shape)
    both = jnp.concatenate([grad_key.reshape(key.shape), grad_value.reshape(key.shape)], axis=1)
    half = width // 2
    away = both[own:].astype(BF)
    away = swap_core(away)
    away = jnp.concatenate(
        [away[:, half:width], away[:, :half], away[:, width + half :], away[:, width : width + half]], axis=1
    )
    both = (both[:own] + away.astype(F32)).astype(BF)
    grad_key, grad_value = both[:, :width], both[:, width:]
    grads = [
        mm(grad_query, query_rows, TN),
        mm(grad_key, key_rows, TN),
        mm(grad_value, key_rows, TN),
        grad_out_w,
    ]
    part_query = mm(grad_query, w_query, NN)
    part_key = mm(grad_key, w_key, NN) + mm(grad_value, w_value, NN)
    return grads, part_query, part_key


def gelu(values):
    return jax.nn.gelu(values, approximate=False)


def feed_forward(rows, w_in, w_down):
    hidden = project(rows, w_in)
    active = gelu(hidden).astype(BF)
    return mm(active, w_down, NN), (hidden, active)


def feed_backward(grad, saved, w_in, w_down, rows):
    hidden, active = saved
    grad_b = grad.astype(BF)
    grad_active = mm(grad_b, w_down, NT)
    grad_hidden = jax.vjp(gelu, hidden)[1](grad_active)[0].astype(BF)
    grads = [mm(grad_hidden, rows, TN), mm(active, grad_b, TN)]
    return grads, mm(grad_hidden, w_in, NN)


def per_device(
    source,
    target,
    out_grad,
    src_len,
    tgt_len,
    owners,
    master,
    rotated_first_moment,
    rotated_second_moment,
    stat_left,
    stat_right,
    basis_left,
    basis_right,
    norm_params,
    norm_one,
    norm_two,
):
    tensor_count = lax.axis_size("tensor")
    me = lax.axis_index("tensor")
    core = me & 1
    head_count = HEADS // tensor_count
    col_count = FFB // tensor_count
    capacity = master.shape[1]
    slot_count = capacity * lax.axis_size("dp")
    row_count = source.shape[1]
    block_rows = master.shape[2]
    width = master.shape[3]

    product, gram = before(stat_right[0], basis_right[0])
    gathered = lax.all_gather(master[0].astype(BF), "dp", axis=0, tiled=True)
    slot_of = slot_positions(owners[0], capacity)
    blocks = gathered[slot_of]
    other_blocks = swap_core(blocks)
    extents = [head_count] * 4 + [col_count] * 2 + [head_count] * 8 + [col_count] * 2
    matrices = []
    offset = 0
    for extent in extents:
        matrices.append(
            jnp.concatenate([blocks[offset : offset + extent], other_blocks[offset : offset + extent]], axis=0).reshape(
                2 * extent * block_rows, width
            )
        )
        offset += extent

    chips = tensor_count // 2
    local = lax.iota(jnp.int32, row_count * chips)
    own_pos = (local // row_count) * (2 * row_count) + core * row_count + local % row_count
    other_pos = own_pos + (1 - 2 * core) * row_count
    key_pos = jnp.concatenate([own_pos, other_pos])
    gains = norm_params[0]
    shifts = norm_params[1]
    src_size = src_len[0]
    tgt_size = tgt_len[0]
    total_rows = local.shape[0]
    enc_allowed = jnp.broadcast_to(key_pos[None, :] < src_size, (total_rows, 2 * total_rows))
    dec_allowed = (key_pos[None, :] <= own_pos[:, None]) & (key_pos[None, :] < tgt_size)
    keep_rows = (own_pos < tgt_size).astype(F32)[:, None]

    src = gather_chips(source[0])
    tgt = gather_chips(target[0])
    cot = gather_chips(out_grad[0])

    branch_one, saved_one = attention_forward(src, src, matrices[0:4], enc_allowed, block_rows)
    z_one = src.astype(F32) + sum_chips(branch_one)
    h_one, pull_one = jax.vjp(layer_norm, z_one, gains[0], shifts[0])
    h_one_b = h_one.astype(BF)
    branch_two, saved_two = feed_forward(h_one_b, matrices[4], matrices[5])
    z_two = h_one + sum_chips(branch_two)
    encoded, pull_two = jax.vjp(layer_norm, z_two, gains[1], shifts[1])
    encoded_b = encoded.astype(BF)
    branch_three, saved_three = attention_forward(tgt, tgt, matrices[6:10], dec_allowed, block_rows)
    z_three = tgt.astype(F32) + sum_chips(branch_three)
    g_one, pull_three = jax.vjp(layer_norm, z_three, gains[2], shifts[2])
    g_one_b = g_one.astype(BF)
    branch_four, saved_four = attention_forward(g_one_b, encoded_b, matrices[10:14], enc_allowed, block_rows)
    z_four = g_one + sum_chips(branch_four)
    g_two, pull_four = jax.vjp(layer_norm, z_four, gains[3], shifts[3])
    g_two_b = g_two.astype(BF)
    branch_five, saved_five = feed_forward(g_two_b, matrices[14], matrices[15])
    z_five = g_two + sum_chips(branch_five)
    normed, pull_five = jax.vjp(layer_norm, z_five, gains[4], shifts[4])
    decoded = own_rows((normed * keep_rows).astype(BF))

    grad_z_five, gain_five, shift_five = pull_five(cot.astype(F32) * keep_rows)
    weights_five, rows_five = feed_backward(grad_z_five, saved_five, matrices[14], matrices[15], g_two_b)
    grad_z_four, gain_four, shift_four = pull_four(grad_z_five + sum_chips(rows_five))
    weights_four, query_four, key_four = attention_backward(
        grad_z_four, saved_four, matrices[10:14], g_one_b, encoded_b, enc_allowed, block_rows
    )
    grad_encoded = sum_chips(key_four)
    grad_z_three, gain_three, shift_three = pull_three(grad_z_four + sum_chips(query_four))
    weights_three, query_three, key_three = attention_backward(
        grad_z_three, saved_three, matrices[6:10], tgt, tgt, dec_allowed, block_rows
    )
    tgt_grad = own_rows(grad_z_three) + sum_chips_own(query_three + key_three)
    grad_z_two, gain_two, shift_two = pull_two(grad_encoded)
    weights_two, rows_two = feed_backward(grad_z_two, saved_two, matrices[4], matrices[5], h_one_b)
    grad_z_one, gain_one, shift_one = pull_one(grad_z_two + sum_chips(rows_two))
    weights_one, query_one, key_one = attention_backward(
        grad_z_one, saved_one, matrices[0:4], src, src, enc_allowed, block_rows
    )
    src_grad = own_rows(grad_z_one) + sum_chips_own(query_one + key_one)

    def reduce_core(grads):
        mine, away = [], []
        for item in grads:
            half = item.shape[0] // 2
            mine.append(item[:half].reshape(-1, block_rows, width))
            away.append(item[half:].reshape(-1, block_rows, width))
        other = swap_core(jnp.concatenate(away, axis=0).astype(BF))
        return (jnp.concatenate(mine, axis=0) + other.astype(F32)).astype(BF)

    block_grad = jnp.concatenate(
        [reduce_core(item) for item in (weights_one, weights_two, weights_three, weights_four, weights_five)], axis=0
    )
    norm_local = jnp.stack(
        [
            jnp.stack([gain_one, gain_two, gain_three, gain_four, gain_five]),
            jnp.stack([shift_one, shift_two, shift_three, shift_four, shift_five]),
        ]
    )
    held = slot_of[None, :] == jnp.arange(slot_count, dtype=jnp.int32)[:, None]
    block_of = jnp.sum(jnp.where(held, jnp.arange(slot_of.shape[0], dtype=jnp.int32)[None, :], 0), axis=1)
    used = jnp.any(held, axis=1)
    in_slots = jnp.where(used[:, None, None], block_grad[block_of], 0)
    own_grad = lax.psum_scatter(in_slots, "dp", scatter_dimension=0, tiled=True)
    norm_grad = sum_everywhere(norm_local)
    results = after(
        own_grad,
        master[0],
        rotated_first_moment[0],
        rotated_second_moment[0],
        stat_left[0],
        basis_left[0],
        stat_right[0],
        basis_right[0],
        product,
        gram,
    )
    norm_one_new = 0.9 * norm_one + 0.1 * norm_grad
    norm_two_new = 0.999 * norm_two + 0.001 * norm_grad * norm_grad
    norm_new = norm_params - rate_vector * (norm_one_new / FIX_ONE) / (jnp.sqrt(norm_two_new / FIX_TWO) + 1e-08)
    return (
        decoded[None],
        src_grad[None],
        tgt_grad[None],
        results[0][None],
        results[1][None],
        results[2][None],
        results[3][None],
        results[4][None],
        results[5][None],
        results[6][None],
        results[7][None],
        norm_new,
        norm_one_new,
        norm_two_new,
    )


def solution(mesh):
    in_specs = (
        P("dp", "tensor", None),
        P("dp", "tensor", None),
        P("dp", "tensor", None),
        P("dp"),
        P("dp"),
        P("tensor", None),
        P("tensor", "dp", None, None),
        P("tensor", "dp", None, None),
        P("tensor", "dp", None, None),
        P("tensor", "dp", None, None),
        P("tensor", "dp", None, None),
        P("tensor", "dp", None, None),
        P("tensor", "dp", None, None),
        P(),
        P(),
        P(),
    )
    out_specs = (
        P("dp", "tensor", None),
        P("dp", "tensor", None),
        P("dp", "tensor", None),
        P("tensor", "dp", None, None),
        P("tensor", "dp", None, None),
        P("tensor", "dp", None, None),
        P("tensor", "dp", None, None),
        P("tensor", "dp", None, None),
        P("tensor", "dp", None, None),
        P("tensor", "dp", None, None),
        P("tensor", "dp", None, None),
        P(),
        P(),
        P(),
    )
    return jax.shard_map(
        per_device, mesh=mesh, in_specs=in_specs, out_specs=out_specs, check_vma=False
    )
```

```python
import jax
import jax.numpy as jnp
from jax import lax
from jax.experimental import pallas as pl
from jax.experimental.pallas import tpu as pltpu
from jax.sharding import PartitionSpec as P

HEADS = 8
STEP = 10
FFB = 32


highest = lax.Precision.HIGHEST
rate_matrix = 0.3
rate_vector = 0.6


def slot_positions(owner_row, capacity):
    block_ids = jnp.arange(owner_row.shape[0], dtype=jnp.int32)
    same_owner = (owner_row[:, None] == owner_row[None, :]).astype(jnp.int32)
    earlier = (block_ids[None, :] < block_ids[:, None]).astype(jnp.int32)
    rank_of = jnp.sum(same_owner * earlier, axis=1)
    return owner_row * capacity + rank_of


def layer_norm(values, norm_gain, norm_shift):
    center = values - jnp.mean(values, axis=-1, keepdims=True)
    spread = jnp.mean(center * center, axis=-1, keepdims=True)
    return center * lax.rsqrt(spread + 1e-05) * norm_gain + norm_shift


F32 = jnp.float32
BF = jnp.bfloat16
NN = (((1,), (0,)), ((), ()))
NT = (((1,), (1,)), ((), ()))
TN = (((0,), (0,)), ((), ()))
FIX_ONE = 1.0 - 0.9**STEP
FIX_TWO = 1.0 - 0.999**STEP


def split(v):
    hi = v.astype(BF)
    return hi, (v - hi.astype(F32)).astype(BF)


def mm(a, b, dims):
    return lax.dot_general(a, b, dims, preferred_element_type=F32)


def mm3(a, b, dims):
    ah, al = a if isinstance(a, tuple) else split(a)
    bh, bl = b if isinstance(b, tuple) else split(b)
    return mm(ah, bh, dims) + (mm(ah, bl, dims) + mm(al, bh, dims))


def before_kernel(s_ref, q_ref, a_ref, m_ref):
    half = s_ref.shape[1] // 2
    q = split(q_ref[0])
    a = 0.95 * mm3(s_ref[0], q, NN)
    a_ref[0] = a
    ah, al = split(a)
    m_ref[0, :half, :] = mm3((ah[:, :half], al[:, :half]), (ah, al), TN)
    m_ref[0, half:, half:] = mm3((ah[:, half:], al[:, half:]), (ah[:, half:], al[:, half:]), TN)


def before(stat, basis, start, n):
    w = stat.shape[1]
    take = pl.BlockSpec((1, w, w), lambda i: (i + start, 0, 0))
    spec = pl.BlockSpec((1, w, w), lambda i: (i, 0, 0))
    return pl.pallas_call(
        before_kernel,
        grid=(n,),
        in_specs=[take, take],
        out_specs=[spec, spec],
        out_shape=[jax.ShapeDtypeStruct((n, w, w), F32)] * 2,
        compiler_params=pltpu.CompilerParams(vmem_limit_bytes=60 << 20),
        cost_estimate=pl.CostEstimate(flops=n * 12 * w**3, bytes_accessed=n * 16 * w * w, transcendentals=0),
        name="before",
    )(stat, basis)


PANEL = 16
BLOCK = 128


def reciprocal(v):
    guess = pl.reciprocal(v, approx=True)
    for _ in range(2):
        guess = guess * (2.0 - v * guess)
    return guess


def factor_panels(dm, dw, pm, pw, um, uw, n, panels):
    size = BLOCK
    end = panels * PANEL
    for s in range(n):
        pm[s * PANEL : s * PANEL + PANEL, :] = dm[s * size : s * size + PANEL, :]
        pw[s * PANEL : s * PANEL + PANEL, :] = dw[s * size : s * size + PANEL, :]
    for p in range(panels):
        top = p * PANEL
        low = top + PANEL
        rows = [pm[pl.ds(a, n, stride=PANEL), :] for a in range(PANEL)]
        eyes = [pw[pl.ds(a, n, stride=PANEL), :] for a in range(PANEL)]
        corner = {}
        for a in range(PANEL):
            for b in range(a, PANEL):
                corner[a, b] = jnp.broadcast_to(rows[a][:, top + b : top + b + 1], (n, size))
        for r in range(PANEL):
            inverse = reciprocal(corner[r, r])
            for a in range(r + 1, PANEL):
                factor = corner[r, a] * inverse
                for b in range(a, PANEL):
                    corner[a, b] = corner[a, b] - factor * corner[r, b]
                rows[a] = rows[a] - factor * rows[r]
                eyes[a] = eyes[a] - factor * eyes[r]
            scale = lax.rsqrt(corner[r, r])
            um[pl.ds(r, n, stride=PANEL), :] = rows[r] * scale
            uw[pl.ds(r, n, stride=PANEL), :] = eyes[r] * scale
        pending = []
        for s in range(n):
            base = s * size
            upper = um[s * PANEL : s * PANEL + PANEL, :]
            lower = uw[s * PANEL : s * PANEL + PANEL, :]
            dw[base + top : base + low, :] = lower
            if low < end:
                uh, ul = split(upper)
                lh, ll = split(lower)
                lhs = jnp.concatenate([uh, uh, ul], axis=0)
                high = jnp.concatenate([uh, lh], axis=1)
                rest = jnp.concatenate([ul, ll], axis=1)
                rhs = jnp.concatenate([high, rest, high], axis=0)
                u = mm(lhs[:, low : low + PANEL], rhs, TN)
                pm[s * PANEL : s * PANEL + PANEL, :] = dm[base + low : base + low + PANEL, :] - u[:, :size]
                pw[s * PANEL : s * PANEL + PANEL, :] = dw[base + low : base + low + PANEL, :] - u[:, size:]
                if low + PANEL < end:
                    pending.append((base, lhs, rhs))
        for base, lhs, rhs in pending:
            u = mm(lhs[:, low + PANEL : end], rhs, TN)
            lo, hi = base + low + PANEL, base + end
            dm[lo:hi, :] = dm[lo:hi, :] - u[:, :size]
            dw[lo:hi, :] = dw[lo:hi, :] - u[:, size:]


def after_kernel(
    g_ref, w_ref, m1_ref, m2_ref, l_ref, ql_ref, s_ref, q_ref, ae_ref, me_ref, al_ref, ml_ref,
    w_out, m1_out, m2_out, l_out, s_out, qln_out, q_out, c_out,
    gram, gram_left, x_left, dm, dw, pm, pw, um, uw,
):
    step = pl.program_id(0)
    count = pl.num_programs(0)
    n = q_out.shape[0]
    width = g_ref.shape[2]
    rows = g_ref.shape[1]
    g = g_ref[0]
    q = split(q_ref[0])
    ql = split(ql_ref[0])
    p = mm(g, q[0], NN) + mm(g, q[1], NN)
    turned = mm3(ql, p, TN)
    first = 0.9 * m1_ref[0] + 0.1 * turned
    second = 0.999 * m2_ref[0] + 0.001 * turned * turned
    m1_out[0] = first
    m2_out[0] = second
    direction = first / FIX_ONE / (jnp.sqrt(second / FIX_TWO) + 1e-08)
    update = mm3(ql, mm3(direction, q, NT), NN)
    weight = w_ref[0]
    weight = weight - rate_matrix * (update + 0.01 * weight)
    w_out[0] = weight
    c_out[0] = weight.astype(BF)
    k = mm(g, g, NT)
    left = 0.95 * l_ref[0] + 0.05 * k
    l_out[0] = left
    s_out[0] = 0.95 * s_ref[0] + 0.05 * mm(g, g, TN)
    early = step < n // 2
    a = jnp.where(early, ae_ref[0], al_ref[0])
    a_parts = split(a)
    b = 0.05 * p
    bh, bl = split(b)
    h = mm(g, a_parts[0], NN) + mm(g, a_parts[1], NN) + 0.5 * mm3(k, (bh, bl), NN)
    q_out[step] = a + mm(jnp.concatenate([g, g], axis=0), jnp.concatenate([bh, bl], axis=0), TN)
    hh, hl = split(h)
    y = jnp.concatenate([hh, bh, hh, bh, hl, bl], axis=0)
    z = jnp.concatenate([bh, hh, bl, hl, bh, hh], axis=0)
    blk = BLOCK
    for i in range(width // blk):
        lo = i * blk
        gram[step, lo : lo + blk, lo:] = jnp.where(early, me_ref[0, lo : lo + blk, lo:], ml_ref[0, lo : lo + blk, lo:]) + mm(y[:, lo : lo + blk], z[:, lo:], TN)
    xl = mm3(left, ql, NN)
    x_left[step] = xl
    gl = mm3(xl, xl, TN)
    gram_left[step] = gl

    @pl.when(step == count - 1)
    def _():
        eye = (lax.broadcasted_iota(jnp.int32, (blk, blk), 0) == lax.broadcasted_iota(jnp.int32, (blk, blk), 1)).astype(F32)
        blocks = width // blk

        def at(s):
            return slice(s * blk, s * blk + blk)

        for s in range(n):
            dm[at(s), :] = eye
            dm[s * blk : s * blk + rows, :rows] = gram_left[s]
            dw[at(s), :] = eye
        factor_panels(dm, dw, pm, pw, um, uw, n, rows // PANEL)
        for s in range(n):
            qln_out[s] = mm3(x_left[s], dw[s * blk : s * blk + rows, :rows], NT)

        def block_step(kk, carry):
            for kb in range(blocks):
                @pl.when(kk == kb)
                def _():
                    for s in range(n):
                        dm[at(s), :] = gram[s, kb * blk : kb * blk + blk, kb * blk : kb * blk + blk]
            for s in range(n):
                dw[at(s), :] = eye
            factor_panels(dm, dw, pm, pw, um, uw, n, blk // PANEL)

            for kb in range(blocks):
                @pl.when(kk == kb)
                def _():
                    lo = kb * blk
                    hi = lo + blk

                    def one(s, c):
                        inv = dw[pl.ds(pl.multiple_of(s * blk, blk), blk), :]
                        gram[s, lo:hi, lo:hi] = inv
                        if blocks == 1:
                            return c
                        ih, il = split(inv)
                        lhs = jnp.concatenate([ih, ih, il], axis=1)

                        def scaled(part):
                            ph, plo = split(part)
                            return mm(lhs, jnp.concatenate([ph, plo, ph], axis=0), NN)

                        if kb > 0:
                            gram[s, lo:hi, :lo] = scaled(gram[s, lo:hi, :lo])
                        if hi < width:
                            up = scaled(gram[s, lo:hi, hi:])
                            uh, ul = split(up)
                            rh, rl = split(gram[s, lo:hi, :hi])
                            us = jnp.concatenate([uh, uh, ul], axis=0)
                            vs = jnp.concatenate([uh, ul, uh], axis=0)
                            rs = jnp.concatenate([rh, rl, rh], axis=0)
                            below = mm(us, rs, TN)
                            if kb > 0:
                                gram[s, hi:, :lo] = gram[s, hi:, :lo] - below[:, :lo]
                            gram[s, hi:, lo:hi] = -below[:, lo:]
                            for i in range(kb + 1, blocks):
                                b0 = i * blk
                                gram[s, b0 : b0 + blk, b0:] = gram[s, b0 : b0 + blk, b0:] - mm(
                                    us[:, b0 - hi : b0 - hi + blk], vs[:, b0 - hi :], TN
                                )
                        return c

                    lax.fori_loop(0, n, one, 0, unroll=min(n, 4))
            return carry

        lax.fori_loop(0, blocks, block_step, 0)

        def finish(s, c):
            x = split(q_out[s])
            for i in range(0, width, 2 * blk):
                hi = i + 2 * blk
                zz = gram[s, i:hi, :hi]
                r_i = lax.broadcasted_iota(jnp.int32, (2 * blk, hi), 0) + i
                c_i = lax.broadcasted_iota(jnp.int32, (2 * blk, hi), 1)
                zz = jnp.where(c_i <= r_i, zz, 0.0)
                q_out[s, :, i:hi] = mm3((x[0][:, :hi], x[1][:, :hi]), zz, NT)
            return c

        lax.fori_loop(0, n, finish, 0, unroll=min(n, 2))


def after(grad, weight, m1, m2, left, ql, stat, q, early, late):
    n, rows, width = weight.shape
    half = n // 2
    first = pl.BlockSpec((1, width, width), lambda i: (jnp.minimum(i, half - 1), 0, 0))
    second = pl.BlockSpec((1, width, width), lambda i: (jnp.maximum(i - half, 0), 0, 0))
    wide = pl.BlockSpec((1, width, width), lambda i: (i, 0, 0))
    flat = pl.BlockSpec((1, rows, width), lambda i: (i, 0, 0))
    small = pl.BlockSpec((1, rows, rows), lambda i: (i, 0, 0))
    sd = jax.ShapeDtypeStruct
    return pl.pallas_call(
        after_kernel,
        grid=(n,),
        in_specs=[flat, flat, flat, flat, small, small, wide, wide, first, first, second, second],
        out_specs=[
            flat, flat, flat, small, wide,
            pl.BlockSpec((n, rows, rows), lambda i: (0, 0, 0)),
            pl.BlockSpec((n, width, width), lambda i: (0, 0, 0)),
            flat,
        ],
        out_shape=[
            sd(weight.shape, F32), sd(weight.shape, F32), sd(weight.shape, F32), sd(left.shape, F32), sd(stat.shape, F32),
            sd(ql.shape, F32), sd(q.shape, F32), sd(weight.shape, BF),
        ],
        scratch_shapes=[
            pltpu.VMEM((n, width, width), F32),
            pltpu.VMEM((n, rows, rows), F32),
            pltpu.VMEM((n, rows, rows), F32),
            pltpu.VMEM((n * BLOCK, BLOCK), F32),
            pltpu.VMEM((n * BLOCK, BLOCK), F32),
            pltpu.VMEM((n * PANEL, BLOCK), F32),
            pltpu.VMEM((n * PANEL, BLOCK), F32),
            pltpu.VMEM((n * PANEL, BLOCK), F32),
            pltpu.VMEM((n * PANEL, BLOCK), F32),
        ],
        compiler_params=pltpu.CompilerParams(vmem_limit_bytes=62 << 20),
        cost_estimate=pl.CostEstimate(flops=n * 12 * width**3, bytes_accessed=n * 24 * width * width, transcendentals=0),
        name="after",
    )(grad, weight, m1, m2, left, ql, stat, q, *early, *late)


def swap_core(values):
    count = lax.axis_size("tensor")
    return lax.ppermute(values, "tensor", [(i, i ^ 1) for i in range(count)])


def chip_bits():
    bit, bits = 2, []
    while bit < lax.axis_size("tensor"):
        bits.append(bit)
        bit *= 2
    return bits


def swap_chip(values, bit):
    count = lax.axis_size("tensor")
    return lax.ppermute(values, "tensor", [(i, i ^ bit) for i in range(count)])


def gather_chips(rows):
    for bit in chip_bits():
        other = swap_chip(rows, bit)
        upper = (lax.axis_index("tensor") & bit) != 0
        rows = jnp.where(
            upper, jnp.concatenate([other, rows], axis=0), jnp.concatenate([rows, other], axis=0)
        )
    return rows


def sum_chips(part):
    for bit in chip_bits():
        part = part.astype(BF)
        part = part.astype(F32) + swap_chip(part, bit).astype(F32)
    return part.astype(F32)


def own_rows(values):
    chips = lax.axis_size("tensor") // 2
    count = values.shape[0] // chips
    return lax.dynamic_slice_in_dim(values, (lax.axis_index("tensor") // 2) * count, count, 0)


def sum_chips_own(part):
    for bit in reversed(chip_bits()):
        half = part.shape[0] // 2
        upper = (lax.axis_index("tensor") & bit) != 0
        keep = jnp.where(upper, part[half:], part[:half])
        give = jnp.where(upper, part[:half], part[half:]).astype(BF)
        part = keep.astype(F32) + swap_chip(give, bit).astype(F32)
    return part


def sum_everywhere(values):
    values = values + swap_core(values)
    count = lax.axis_size("dp")
    if count & (count - 1):
        return lax.psum(values, "dp")
    bit = 1
    while bit < count:
        values = values + lax.ppermute(values, "dp", [(i, i ^ bit) for i in range(count)])
        bit *= 2
    return values


def shift(values, axis, pairs):
    return lax.ppermute(values, axis, pairs)


def gather_owners(own, beside):
    count = lax.axis_size("dp")
    if count != 8:
        return lax.all_gather(own, "dp", axis=0, tiled=True), [make() for make in beside]
    across = [(i, i ^ 1) for i in range(8)]
    z = lax.axis_index("dp") // 2
    even = (z & 1) == 0
    ups, downs, far = [own], [own], []
    made = []
    for s in range(4):
        if s == 0:
            pay = own
        elif s == 1:
            pay = jnp.where(even, downs[1], ups[1])
        elif s == 2:
            pay = jnp.where(z == 0, downs[2], jnp.where(z == 1, downs[1], jnp.where(z == 2, ups[1], ups[2])))
        else:
            pay = jnp.where(z == 0, downs[3], jnp.where(z == 1, downs[2], jnp.where(z == 2, ups[2], ups[3])))
        moved = [shift(pay, "dp", across)]
        if s < 3:
            moved.append(shift(ups[s], "dp", [(i, i + 2) for i in range(2 * s, 6)]))
            moved.append(shift(downs[s], "dp", [(i, i - 2) for i in range(2, 8 - 2 * s)]))
        extra = [beside[s]()] if s < len(beside) else []
        moved, extra = lax.optimization_barrier((moved, extra))
        made.extend(extra)
        far.append(moved[0])
        if s < 3:
            ups.append(moved[1])
            downs.append(moved[2])
    far_rel = [
        far[0],
        jnp.where(z == 0, far[3], jnp.where(z == 1, far[1], jnp.where(z == 2, far[2], far[1]))),
        jnp.where(z == 0, far[2], jnp.where(z == 1, far[3], jnp.where(z == 2, far[3], far[2]))),
        jnp.where(z == 0, far[1], jnp.where(z == 1, far[2], jnp.where(z == 2, far[1], far[3]))),
    ]
    parts = [own, far_rel[0]]
    for s in range(1, 4):
        parts.append(ups[s] + downs[4 - s])
        parts.append(far_rel[s])
    return jnp.concatenate(parts, axis=0), made


def owner_place(owner):
    if lax.axis_size("dp") != 8:
        return owner
    me = lax.axis_index("dp")
    return ((me // 2 - owner // 2) % 4) * 2 + ((me ^ owner) & 1)


def sum_to_owner(blocks, block_of, capacity):
    if lax.axis_size("dp") != 8:
        return lax.psum_scatter(blocks[block_of], "dp", scatter_dimension=0, tiled=True)
    me = lax.axis_index("dp")
    z = me // 2
    order = jnp.array([[3, 2, 1, 0], [3, 2, 0, 1], [0, 1, 3, 2], [0, 1, 2, 3]], jnp.int32)[z]
    table = block_of.reshape(8, capacity)
    give = blocks[table[order * 2 + ((me & 1) ^ 1)].reshape(-1)].reshape((4, capacity) + blocks.shape[1:])
    keep = blocks[table[order * 2 + (me & 1)].reshape(-1)].reshape((4, capacity) + blocks.shape[1:])
    across = [(i, i ^ 1) for i in range(8)]
    def swapped(k):
        return shift(give[k], "dp", across)

    def total(k, other):
        return keep[k].astype(F32) + other.astype(F32)

    def send(part, other, direction, step):
        part = (part if other is None else part + other.astype(F32)).astype(BF)
        if direction > 0:
            return shift(part, "dp", [(i, i + 2) for i in range(2 * step)])
        return shift(part, "dp", [(i, i - 2) for i in range(8 - 2 * step, 8)])

    first = total(0, swapped(0))
    moved = lax.optimization_barrier((swapped(1), send(first, None, 1, 1), send(first, None, -1, 1)))
    second = total(1, moved[0])
    up = send(jnp.where(z == 0, second, first), moved[1], 1, 2)
    down = send(jnp.where(z == 3, second, first), moved[2], -1, 2)
    moved = lax.optimization_barrier((swapped(2), up, down))
    third = total(2, moved[0])
    up = send(jnp.where(z == 1, second, third), moved[1], 1, 3)
    down = send(jnp.where(z == 2, second, third), moved[2], -1, 3)
    moved = lax.optimization_barrier((swapped(3), up, down))
    return (total(3, moved[0]) + moved[1].astype(F32) + moved[2].astype(F32)).astype(BF)


def project(rows, matrix):
    return mm(rows, matrix, NT)


def join_core(own, width):
    other = swap_core(own)
    half = width // 2
    parts = []
    for start in range(0, own.shape[1], width):
        parts.append(other[:, start + half : start + width])
        parts.append(other[:, start : start + half])
    return jnp.concatenate([own, jnp.concatenate(parts, axis=1)], axis=0)


def attention_scores(query, key, allowed):
    scale = query.shape[-1] ** (-0.5)
    scores = jnp.einsum("qhe,khe->hqk", query, key, preferred_element_type=F32) * scale
    return jnp.where(allowed[None], scores, -1e30)


def heads_of(rows, size):
    return rows.reshape(rows.shape[0], -1, size)


def attention_forward(query_rows, key_rows, weights, allowed, size):
    w_query, w_key, w_value, w_out = weights
    width = w_query.shape[0]
    query = project(query_rows, w_query).astype(BF)
    pair = project(key_rows, jnp.concatenate([w_key, w_value], axis=0)).astype(BF)
    pair = join_core(pair, width)
    key, value = pair[:, :width], pair[:, width:]
    scores = attention_scores(heads_of(query, size), heads_of(key, size), allowed)
    top = jnp.max(scores, axis=-1, keepdims=True)
    powers = jnp.exp(scores - top)
    total = jnp.sum(powers, axis=-1, keepdims=True)
    chance = powers / total
    log_total = top + jnp.log(total)
    mixed = jnp.einsum("hqk,khe->qhe", chance.astype(BF), heads_of(value, size), preferred_element_type=F32)
    mixed = mixed.astype(BF).reshape(query.shape)
    return mm(mixed, w_out, NN), (query, key, value, log_total, mixed)


def attention_backward(grad, saved, weights, query_rows, key_rows, allowed, size):
    w_query, w_key, w_value, w_out = weights
    query, key, value, log_total, mixed = saved
    width = query.shape[1]
    own = key_rows.shape[0]
    grad_b = grad.astype(BF)
    grad_mixed = heads_of(mm(grad_b, w_out, NT).astype(BF), size)
    grad_out_w = mm(mixed, grad_b, TN)
    query_h, key_h, value_h = heads_of(query, size), heads_of(key, size), heads_of(value, size)
    scores = attention_scores(query_h, key_h, allowed)
    chance = jnp.exp(scores - log_total)
    grad_value = jnp.einsum("hqk,qhe->khe", chance.astype(BF), grad_mixed, preferred_element_type=F32)
    grad_chance = jnp.einsum("qhe,khe->hqk", grad_mixed, value_h, preferred_element_type=F32)
    inner = jnp.sum(chance * grad_chance, axis=-1, keepdims=True)
    grad_score = (chance * (grad_chance - inner)).astype(BF)
    scale = size ** (-0.5)
    grad_query = jnp.einsum("hqk,khe->qhe", grad_score, key_h, preferred_element_type=F32) * scale
    grad_key = jnp.einsum("hqk,qhe->khe", grad_score, query_h, preferred_element_type=F32) * scale
    grad_query = grad_query.astype(BF).reshape(query.shape)
    both = jnp.concatenate([grad_key.reshape(key.shape), grad_value.reshape(key.shape)], axis=1)
    half = width // 2
    away = both[own:].astype(BF)
    away = swap_core(away)
    away = jnp.concatenate(
        [away[:, half:width], away[:, :half], away[:, width + half :], away[:, width : width + half]], axis=1
    )
    both = (both[:own] + away.astype(F32)).astype(BF)
    grad_key, grad_value = both[:, :width], both[:, width:]
    grads = [
        mm(grad_query, query_rows, TN),
        mm(grad_key, key_rows, TN),
        mm(grad_value, key_rows, TN),
        grad_out_w,
    ]
    part_query = mm(grad_query, w_query, NN)
    part_key = mm(grad_key, w_key, NN) + mm(grad_value, w_value, NN)
    return grads, part_query, part_key


def gelu(values):
    return jax.nn.gelu(values, approximate=False)


def feed_forward(rows, w_in, w_down):
    hidden = project(rows, w_in)
    active = gelu(hidden).astype(BF)
    return mm(active, w_down, NN), (hidden, active)


def feed_backward(grad, saved, w_in, w_down, rows):
    hidden, active = saved
    grad_b = grad.astype(BF)
    grad_active = mm(grad_b, w_down, NT)
    grad_hidden = jax.vjp(gelu, hidden)[1](grad_active)[0].astype(BF)
    grads = [mm(grad_hidden, rows, TN), mm(active, grad_b, TN)]
    return grads, mm(grad_hidden, w_in, NN)


def per_device(
    source,
    target,
    out_grad,
    src_len,
    tgt_len,
    owners,
    master,
    rotated_first_moment,
    rotated_second_moment,
    stat_left,
    stat_right,
    basis_left,
    basis_right,
    norm_params,
    norm_one,
    norm_two,
):
    tensor_count = lax.axis_size("tensor")
    me = lax.axis_index("tensor")
    core = me & 1
    head_count = HEADS // tensor_count
    col_count = FFB // tensor_count
    capacity = master.shape[1]
    slot_count = capacity * lax.axis_size("dp")
    row_count = source.shape[1]
    block_rows = master.shape[2]
    width = master.shape[3]

    half = max(capacity // 2, 1)
    gathered, made = gather_owners(
        master[0].astype(BF),
        [
            lambda: (before(stat_right[0], basis_right[0], 0, half), gather_chips(source[0])),
            lambda: (before(stat_right[0], basis_right[0], half, capacity - half), gather_chips(target[0])),
            lambda: gather_chips(out_grad[0]),
        ],
    )
    (early, src), (late, tgt), cot = made
    slot_of = slot_positions(owners[0], capacity)
    blocks = gathered[owner_place(slot_of // capacity) * capacity + slot_of % capacity]
    other_blocks = swap_core(blocks)
    extents = [head_count] * 4 + [col_count] * 2 + [head_count] * 8 + [col_count] * 2
    matrices = []
    offset = 0
    for extent in extents:
        matrices.append(
            jnp.concatenate([blocks[offset : offset + extent], other_blocks[offset : offset + extent]], axis=0).reshape(
                2 * extent * block_rows, width
            )
        )
        offset += extent

    chips = tensor_count // 2
    local = lax.iota(jnp.int32, row_count * chips)
    own_pos = (local // row_count) * (2 * row_count) + core * row_count + local % row_count
    other_pos = own_pos + (1 - 2 * core) * row_count
    key_pos = jnp.concatenate([own_pos, other_pos])
    gains = norm_params[0]
    shifts = norm_params[1]
    src_size = src_len[0]
    tgt_size = tgt_len[0]
    total_rows = local.shape[0]
    enc_allowed = jnp.broadcast_to(key_pos[None, :] < src_size, (total_rows, 2 * total_rows))
    dec_allowed = (key_pos[None, :] <= own_pos[:, None]) & (key_pos[None, :] < tgt_size)
    keep_rows = (own_pos < tgt_size).astype(F32)[:, None]

    branch_one, saved_one = attention_forward(src, src, matrices[0:4], enc_allowed, block_rows)
    z_one = src.astype(F32) + sum_chips(branch_one)
    h_one, pull_one = jax.vjp(layer_norm, z_one, gains[0], shifts[0])
    h_one_b = h_one.astype(BF)
    branch_two, saved_two = feed_forward(h_one_b, matrices[4], matrices[5])
    z_two = h_one + sum_chips(branch_two)
    encoded, pull_two = jax.vjp(layer_norm, z_two, gains[1], shifts[1])
    encoded_b = encoded.astype(BF)
    branch_three, saved_three = attention_forward(tgt, tgt, matrices[6:10], dec_allowed, block_rows)
    z_three = tgt.astype(F32) + sum_chips(branch_three)
    g_one, pull_three = jax.vjp(layer_norm, z_three, gains[2], shifts[2])
    g_one_b = g_one.astype(BF)
    branch_four, saved_four = attention_forward(g_one_b, encoded_b, matrices[10:14], enc_allowed, block_rows)
    z_four = g_one + sum_chips(branch_four)
    g_two, pull_four = jax.vjp(layer_norm, z_four, gains[3], shifts[3])
    g_two_b = g_two.astype(BF)
    branch_five, saved_five = feed_forward(g_two_b, matrices[14], matrices[15])
    z_five = g_two + sum_chips(branch_five)
    normed, pull_five = jax.vjp(layer_norm, z_five, gains[4], shifts[4])
    decoded = own_rows((normed * keep_rows).astype(BF))

    grad_z_five, gain_five, shift_five = pull_five(cot.astype(F32) * keep_rows)
    weights_five, rows_five = feed_backward(grad_z_five, saved_five, matrices[14], matrices[15], g_two_b)
    grad_z_four, gain_four, shift_four = pull_four(grad_z_five + sum_chips(rows_five))
    weights_four, query_four, key_four = attention_backward(
        grad_z_four, saved_four, matrices[10:14], g_one_b, encoded_b, enc_allowed, block_rows
    )
    grad_encoded = sum_chips(key_four)
    grad_z_three, gain_three, shift_three = pull_three(grad_z_four + sum_chips(query_four))
    weights_three, query_three, key_three = attention_backward(
        grad_z_three, saved_three, matrices[6:10], tgt, tgt, dec_allowed, block_rows
    )
    tgt_grad = own_rows(grad_z_three) + sum_chips_own(query_three + key_three)
    grad_z_two, gain_two, shift_two = pull_two(grad_encoded)
    weights_two, rows_two = feed_backward(grad_z_two, saved_two, matrices[4], matrices[5], h_one_b)
    grad_z_one, gain_one, shift_one = pull_one(grad_z_two + sum_chips(rows_two))
    weights_one, query_one, key_one = attention_backward(
        grad_z_one, saved_one, matrices[0:4], src, src, enc_allowed, block_rows
    )
    src_grad = own_rows(grad_z_one) + sum_chips_own(query_one + key_one)

    def reduce_core(grads):
        mine, away = [], []
        for item in grads:
            half = item.shape[0] // 2
            mine.append(item[:half].reshape(-1, block_rows, width))
            away.append(item[half:].reshape(-1, block_rows, width))
        other = swap_core(jnp.concatenate(away, axis=0).astype(BF))
        return (jnp.concatenate(mine, axis=0) + other.astype(F32)).astype(BF)

    block_grad = jnp.concatenate(
        [reduce_core(item) for item in (weights_one, weights_two, weights_three, weights_four, weights_five)]
        + [jnp.zeros((1, block_rows, width), BF)],
        axis=0,
    )
    norm_local = jnp.stack(
        [
            jnp.stack([gain_one, gain_two, gain_three, gain_four, gain_five]),
            jnp.stack([shift_one, shift_two, shift_three, shift_four, shift_five]),
        ]
    )
    held = slot_of[None, :] == jnp.arange(slot_count, dtype=jnp.int32)[:, None]
    block_of = jnp.sum(jnp.where(held, jnp.arange(slot_of.shape[0], dtype=jnp.int32)[None, :], 0), axis=1)
    block_of = jnp.where(jnp.any(held, axis=1), block_of, slot_of.shape[0])
    own_grad = sum_to_owner(block_grad, block_of, capacity)
    norm_grad = sum_everywhere(norm_local)
    results = after(
        own_grad,
        master[0],
        rotated_first_moment[0],
        rotated_second_moment[0],
        stat_left[0],
        basis_left[0],
        stat_right[0],
        basis_right[0],
        early,
        late,
    )
    norm_one_new = 0.9 * norm_one + 0.1 * norm_grad
    norm_two_new = 0.999 * norm_two + 0.001 * norm_grad * norm_grad
    norm_new = norm_params - rate_vector * (norm_one_new / FIX_ONE) / (jnp.sqrt(norm_two_new / FIX_TWO) + 1e-08)
    return (
        decoded[None],
        src_grad[None],
        tgt_grad[None],
        results[0][None],
        results[1][None],
        results[2][None],
        results[3][None],
        results[4][None],
        results[5][None],
        results[6][None],
        results[7][None],
        norm_new,
        norm_one_new,
        norm_two_new,
    )


def solution(mesh):
    in_specs = (
        P("dp", "tensor", None),
        P("dp", "tensor", None),
        P("dp", "tensor", None),
        P("dp"),
        P("dp"),
        P("tensor", None),
        P("tensor", "dp", None, None),
        P("tensor", "dp", None, None),
        P("tensor", "dp", None, None),
        P("tensor", "dp", None, None),
        P("tensor", "dp", None, None),
        P("tensor", "dp", None, None),
        P("tensor", "dp", None, None),
        P(),
        P(),
        P(),
    )
    out_specs = (
        P("dp", "tensor", None),
        P("dp", "tensor", None),
        P("dp", "tensor", None),
        P("tensor", "dp", None, None),
        P("tensor", "dp", None, None),
        P("tensor", "dp", None, None),
        P("tensor", "dp", None, None),
        P("tensor", "dp", None, None),
        P("tensor", "dp", None, None),
        P("tensor", "dp", None, None),
        P("tensor", "dp", None, None),
        P(),
        P(),
        P(),
    )
    return jax.shard_map(
        per_device, mesh=mesh, in_specs=in_specs, out_specs=out_specs, check_vma=False
    )
```

```python
import functools
import math

import jax
import jax.numpy as jnp
from jax import lax
from jax.experimental import pallas as pl
from jax.experimental.pallas import tpu as pltpu
from jax.sharding import PartitionSpec as P

HEADS = 8
STEP = 10
FFB = 32


highest = lax.Precision.HIGHEST
rate_matrix = 0.3
rate_vector = 0.6


def slot_positions(owner_row, capacity):
    block_ids = jnp.arange(owner_row.shape[0], dtype=jnp.int32)
    same_owner = (owner_row[:, None] == owner_row[None, :]).astype(jnp.int32)
    earlier = (block_ids[None, :] < block_ids[:, None]).astype(jnp.int32)
    rank_of = jnp.sum(same_owner * earlier, axis=1)
    return owner_row * capacity + rank_of


def layer_norm(values, norm_gain, norm_shift):
    center = values - jnp.mean(values, axis=-1, keepdims=True)
    spread = jnp.mean(center * center, axis=-1, keepdims=True)
    return center * lax.rsqrt(spread + 1e-05) * norm_gain + norm_shift


F32 = jnp.float32
BF = jnp.bfloat16
NN = (((1,), (0,)), ((), ()))
NT = (((1,), (1,)), ((), ()))
TN = (((0,), (0,)), ((), ()))
FIX_ONE = 1.0 - 0.9**STEP
FIX_TWO = 1.0 - 0.999**STEP


def split(v):
    hi = v.astype(BF)
    return hi, (v - hi.astype(F32)).astype(BF)


def mm(a, b, dims):
    return lax.dot_general(a, b, dims, preferred_element_type=F32)


def mm3(a, b, dims):
    ah, al = a if isinstance(a, tuple) else split(a)
    bh, bl = b if isinstance(b, tuple) else split(b)
    return mm(ah, bh, dims) + (mm(ah, bl, dims) + mm(al, bh, dims))


def before_kernel(s_ref, q_ref, a_ref, m_ref):
    half = s_ref.shape[1] // 2
    q = split(q_ref[0])
    a = 0.95 * mm3(s_ref[0], q, NN)
    a_ref[0] = a
    ah, al = split(a)
    m_ref[0, :half, :] = mm3((ah[:, :half], al[:, :half]), (ah, al), TN)
    m_ref[0, half:, half:] = mm3((ah[:, half:], al[:, half:]), (ah[:, half:], al[:, half:]), TN)


def before(stat, basis, start, n):
    w = stat.shape[1]
    take = pl.BlockSpec((1, w, w), lambda i: (i + start, 0, 0))
    spec = pl.BlockSpec((1, w, w), lambda i: (i, 0, 0))
    return pl.pallas_call(
        before_kernel,
        grid=(n,),
        in_specs=[take, take],
        out_specs=[spec, spec],
        out_shape=[pltpu.HBM((n, w, w), F32)] * 2,
        compiler_params=pltpu.CompilerParams(vmem_limit_bytes=24 << 20),
        cost_estimate=pl.CostEstimate(flops=n * 12 * w**3, bytes_accessed=n * 16 * w * w, transcendentals=0),
        name="before",
    )(pltpu.with_memory_space_constraint(stat, pltpu.HBM), pltpu.with_memory_space_constraint(basis, pltpu.HBM))


PANEL = 16
BLOCK = 128


def reciprocal(v):
    guess = pl.reciprocal(v, approx=True)
    for _ in range(2):
        guess = guess * (2.0 - v * guess)
    return guess


def factor_panels(dm, dw, pm, pw, um, uw, n, panels):
    size = BLOCK
    end = panels * PANEL
    for s in range(n):
        pm[s * PANEL : s * PANEL + PANEL, :] = dm[s * size : s * size + PANEL, :]
        pw[s * PANEL : s * PANEL + PANEL, :] = dw[s * size : s * size + PANEL, :]
    for p in range(panels):
        top = p * PANEL
        low = top + PANEL
        rows = [pm[pl.ds(a, n, stride=PANEL), :] for a in range(PANEL)]
        eyes = [pw[pl.ds(a, n, stride=PANEL), :] for a in range(PANEL)]
        corner = {}
        for a in range(PANEL):
            for b in range(a, PANEL):
                corner[a, b] = jnp.broadcast_to(rows[a][:, top + b : top + b + 1], (n, size))
        for r in range(PANEL):
            inverse = reciprocal(corner[r, r])
            for a in range(r + 1, PANEL):
                factor = corner[r, a] * inverse
                for b in range(a, PANEL):
                    corner[a, b] = corner[a, b] - factor * corner[r, b]
                rows[a] = rows[a] - factor * rows[r]
                eyes[a] = eyes[a] - factor * eyes[r]
            scale = lax.rsqrt(corner[r, r])
            um[pl.ds(r, n, stride=PANEL), :] = rows[r] * scale
            uw[pl.ds(r, n, stride=PANEL), :] = eyes[r] * scale
        pending = []
        for s in range(n):
            base = s * size
            upper = um[s * PANEL : s * PANEL + PANEL, :]
            lower = uw[s * PANEL : s * PANEL + PANEL, :]
            dw[base + top : base + low, :] = lower
            if low < end:
                uh, ul = split(upper)
                lh, ll = split(lower)
                lhs = jnp.concatenate([uh, uh, ul], axis=0)
                high = jnp.concatenate([uh, lh], axis=1)
                rest = jnp.concatenate([ul, ll], axis=1)
                rhs = jnp.concatenate([high, rest, high], axis=0)
                u = mm(lhs[:, low : low + PANEL], rhs, TN)
                pm[s * PANEL : s * PANEL + PANEL, :] = dm[base + low : base + low + PANEL, :] - u[:, :size]
                pw[s * PANEL : s * PANEL + PANEL, :] = dw[base + low : base + low + PANEL, :] - u[:, size:]
                if low + PANEL < end:
                    pending.append((base, lhs, rhs))
        for base, lhs, rhs in pending:
            u = mm(lhs[:, low + PANEL : end], rhs, TN)
            lo, hi = base + low + PANEL, base + end
            dm[lo:hi, :] = dm[lo:hi, :] - u[:, :size]
            dw[lo:hi, :] = dw[lo:hi, :] - u[:, size:]


def after_kernel(
    g_ref, w_ref, m1_ref, m2_ref, l_ref, ql_ref, s_ref, q_ref, ae_ref, me_ref, al_ref, ml_ref,
    w_out, m1_out, m2_out, l_out, s_out, qln_out, q_out, c_out,
    gram, gram_left, x_left, dm, dw, pm, pw, um, uw,
):
    step = pl.program_id(0)
    count = pl.num_programs(0)
    n = q_out.shape[0]
    width = g_ref.shape[2]
    rows = g_ref.shape[1]
    per = g_ref.shape[0]
    blk = BLOCK

    def one_slot(i, a_ref, m_ref):
        slot = step * per + i
        g = g_ref[i]
        q = split(q_ref[i])
        ql = split(ql_ref[i])
        p = mm(g, q[0], NN) + mm(g, q[1], NN)
        k = mm(g, g, NT)
        a = a_ref[i]
        a_parts = split(a)
        b = 0.05 * p
        bh, bl = split(b)
        h = mm(g, a_parts[0], NN) + mm(g, a_parts[1], NN) + 0.5 * mm3(k, (bh, bl), NN)
        q_out[slot] = a + mm(jnp.concatenate([g, g], axis=0), jnp.concatenate([bh, bl], axis=0), TN)
        hh, hl = split(h)
        y = jnp.concatenate([hh, bh, hh, bh, hl, bl], axis=0)
        z = jnp.concatenate([bh, hh, bl, hl, bh, hh], axis=0)
        for j in range(width // blk):
            lo = j * blk
            gram[slot, lo : lo + blk, lo:] = m_ref[i, lo : lo + blk, lo:] + mm(y[:, lo : lo + blk], z[:, lo:], TN)
        left = 0.95 * l_ref[i] + 0.05 * k
        l_out[i] = left
        xl = mm3(left, ql, NN)
        x_left[slot] = xl
        gram_left[slot] = mm3(xl, xl, TN)
        s_out[i] = 0.95 * s_ref[i] + 0.05 * mm(g, g, TN)
        turned = mm3(ql, p, TN)
        first = 0.9 * m1_ref[i] + 0.1 * turned
        second = 0.999 * m2_ref[i] + 0.001 * turned * turned
        m1_out[i] = first
        m2_out[i] = second
        direction = first / FIX_ONE / (jnp.sqrt(second / FIX_TWO) + 1e-08)
        update = mm3(ql, mm3(direction, q, NT), NN)
        weight = w_ref[i]
        weight = weight - rate_matrix * (update + 0.01 * weight)
        w_out[i] = weight
        c_out[i] = weight.astype(BF)

    @pl.when(step * per < n // 2)
    def _():
        for i in range(per):
            one_slot(i, ae_ref, me_ref)

    @pl.when(step * per >= n // 2)
    def _():
        for i in range(per):
            one_slot(i, al_ref, ml_ref)

    @pl.when(step == count - 1)
    def _():
        eye = (lax.broadcasted_iota(jnp.int32, (blk, blk), 0) == lax.broadcasted_iota(jnp.int32, (blk, blk), 1)).astype(F32)
        blocks = width // blk

        def at(s):
            return slice(s * blk, s * blk + blk)

        for s in range(n):
            dm[at(s), :] = eye
            dm[s * blk : s * blk + rows, :rows] = gram_left[s]
            dw[at(s), :] = eye
        factor_panels(dm, dw, pm, pw, um, uw, n, rows // PANEL)
        for s in range(n):
            qln_out[s] = mm3(x_left[s], dw[s * blk : s * blk + rows, :rows], NT)

        def block_step(kk, carry):
            for kb in range(blocks):
                @pl.when(kk == kb)
                def _():
                    for s in range(n):
                        dm[at(s), :] = gram[s, kb * blk : kb * blk + blk, kb * blk : kb * blk + blk]
            for s in range(n):
                dw[at(s), :] = eye
            factor_panels(dm, dw, pm, pw, um, uw, n, blk // PANEL)

            for kb in range(blocks):
                @pl.when(kk == kb)
                def _():
                    lo = kb * blk
                    hi = lo + blk

                    def one(s, c):
                        inv = dw[pl.ds(pl.multiple_of(s * blk, blk), blk), :]
                        gram[s, lo:hi, lo:hi] = inv
                        if blocks == 1:
                            return c
                        ih, il = split(inv)
                        lhs = jnp.concatenate([ih, ih, il], axis=1)

                        def scaled(part):
                            ph, plo = split(part)
                            return mm(lhs, jnp.concatenate([ph, plo, ph], axis=0), NN)

                        if kb > 0:
                            gram[s, lo:hi, :lo] = scaled(gram[s, lo:hi, :lo])
                        if hi < width:
                            up = scaled(gram[s, lo:hi, hi:])
                            uh, ul = split(up)
                            rh, rl = split(gram[s, lo:hi, :hi])
                            us = jnp.concatenate([uh, uh, ul], axis=0)
                            vs = jnp.concatenate([uh, ul, uh], axis=0)
                            rs = jnp.concatenate([rh, rl, rh], axis=0)
                            below = mm(us, rs, TN)
                            if kb > 0:
                                gram[s, hi:, :lo] = gram[s, hi:, :lo] - below[:, :lo]
                            gram[s, hi:, lo:hi] = -below[:, lo:]
                            for i in range(kb + 1, blocks):
                                b0 = i * blk
                                gram[s, b0 : b0 + blk, b0:] = gram[s, b0 : b0 + blk, b0:] - mm(
                                    us[:, b0 - hi : b0 - hi + blk], vs[:, b0 - hi :], TN
                                )
                        return c

                    lax.fori_loop(0, n, one, 0, unroll=min(n, 4))
            return carry

        lax.fori_loop(0, blocks, block_step, 0)

        def finish(s, c):
            x = split(q_out[s])
            for i in range(0, width, 2 * blk):
                hi = i + 2 * blk
                zz = gram[s, i:hi, :hi]
                r_i = lax.broadcasted_iota(jnp.int32, (2 * blk, hi), 0) + i
                c_i = lax.broadcasted_iota(jnp.int32, (2 * blk, hi), 1)
                zz = jnp.where(c_i <= r_i, zz, 0.0)
                q_out[s, :, i:hi] = mm3((x[0][:, :hi], x[1][:, :hi]), zz, NT)
            return c

        lax.fori_loop(0, n, finish, 0, unroll=min(n, 2))


def after(grad, weight, m1, m2, left, ql, stat, q, early, late):
    n, rows, width = weight.shape
    per = 2 if n % 4 == 0 else 1
    half = n // 2 // per
    first = pl.BlockSpec((per, width, width), lambda i: (jnp.minimum(i, half - 1), 0, 0))
    second = pl.BlockSpec((per, width, width), lambda i: (jnp.maximum(i - half, 0), 0, 0))
    wide = pl.BlockSpec((per, width, width), lambda i: (i, 0, 0))
    flat = pl.BlockSpec((per, rows, width), lambda i: (i, 0, 0))
    small = pl.BlockSpec((per, rows, rows), lambda i: (i, 0, 0))
    sd = jax.ShapeDtypeStruct
    return pl.pallas_call(
        after_kernel,
        grid=(n // per,),
        in_specs=[flat, flat, flat, flat, small, small, wide, wide, first, first, second, second],
        out_specs=[
            flat, flat, flat, small, wide,
            pl.BlockSpec((n, rows, rows), lambda i: (0, 0, 0)),
            pl.BlockSpec((n, width, width), lambda i: (0, 0, 0)),
            flat,
        ],
        out_shape=[
            sd(weight.shape, F32), sd(weight.shape, F32), sd(weight.shape, F32), sd(left.shape, F32), sd(stat.shape, F32),
            sd(ql.shape, F32), sd(q.shape, F32), sd(weight.shape, BF),
        ],
        scratch_shapes=[
            pltpu.VMEM((n, width, width), F32),
            pltpu.VMEM((n, rows, rows), F32),
            pltpu.VMEM((n, rows, rows), F32),
            pltpu.VMEM((n * BLOCK, BLOCK), F32),
            pltpu.VMEM((n * BLOCK, BLOCK), F32),
            pltpu.VMEM((n * PANEL, BLOCK), F32),
            pltpu.VMEM((n * PANEL, BLOCK), F32),
            pltpu.VMEM((n * PANEL, BLOCK), F32),
            pltpu.VMEM((n * PANEL, BLOCK), F32),
        ],
        compiler_params=pltpu.CompilerParams(vmem_limit_bytes=62 << 20),
        cost_estimate=pl.CostEstimate(flops=n * 12 * width**3, bytes_accessed=n * 24 * width * width, transcendentals=0),
        name="after",
    )(grad, weight, m1, m2, left, ql, stat, q, *early, *late)


def swap_core(values):
    count = lax.axis_size("tensor")
    return lax.ppermute(values, "tensor", [(i, i ^ 1) for i in range(count)])


def chip_bits():
    bit, bits = 2, []
    while bit < lax.axis_size("tensor"):
        bits.append(bit)
        bit *= 2
    return bits


def swap_chip(values, bit):
    count = lax.axis_size("tensor")
    return lax.ppermute(values, "tensor", [(i, i ^ bit) for i in range(count)])


def gather_chips(rows):
    for bit in chip_bits():
        other = swap_chip(rows, bit)
        upper = (lax.axis_index("tensor") & bit) != 0
        rows = jnp.where(
            upper, jnp.concatenate([other, rows], axis=0), jnp.concatenate([rows, other], axis=0)
        )
    return rows


def sum_chips(part):
    for bit in chip_bits():
        part = part.astype(BF)
        part = part.astype(F32) + swap_chip(part, bit).astype(F32)
    return part.astype(F32)


def own_rows(values):
    chips = lax.axis_size("tensor") // 2
    count = values.shape[0] // chips
    return lax.dynamic_slice_in_dim(values, (lax.axis_index("tensor") // 2) * count, count, 0)


def sum_chips_own(part):
    for bit in reversed(chip_bits()):
        half = part.shape[0] // 2
        upper = (lax.axis_index("tensor") & bit) != 0
        keep = jnp.where(upper, part[half:], part[:half])
        give = jnp.where(upper, part[:half], part[half:]).astype(BF)
        part = keep.astype(F32) + swap_chip(give, bit).astype(F32)
    return part


def sum_everywhere(values):
    values = values + swap_core(values)
    count = lax.axis_size("dp")
    if count & (count - 1):
        return lax.psum(values, "dp")
    bit = 1
    while bit < count:
        values = values + lax.ppermute(values, "dp", [(i, i ^ bit) for i in range(count)])
        bit *= 2
    return values


def shift(values, axis, pairs):
    return lax.ppermute(values, axis, pairs)


def gather_owners(own, beside):
    count = lax.axis_size("dp")
    if count != 8:
        return [lax.all_gather(own, "dp", axis=0, tiled=True)], [make() for make in beside]
    across = [(i, i ^ 1) for i in range(8)]
    z = lax.axis_index("dp") // 2
    even = (z & 1) == 0
    ups, downs, far = [own], [own], []
    made = []
    for s in range(4):
        if s == 0:
            pay = own
        elif s == 1:
            pay = jnp.where(even, downs[1], ups[1])
        elif s == 2:
            pay = jnp.where(z == 0, downs[2], jnp.where(z == 1, downs[1], jnp.where(z == 2, ups[1], ups[2])))
        else:
            pay = jnp.where(z == 0, downs[3], jnp.where(z == 1, downs[2], jnp.where(z == 2, ups[2], ups[3])))
        moved = [shift(pay, "dp", across)]
        if s < 3:
            moved.append(shift(ups[s], "dp", [(i, i + 2) for i in range(2 * s, 6)]))
            moved.append(shift(downs[s], "dp", [(i, i - 2) for i in range(2, 8 - 2 * s)]))
        extra = [beside[s]()] if s < len(beside) else []
        moved, extra = lax.optimization_barrier((moved, extra))
        made.extend(extra)
        far.append(moved[0])
        if s < 3:
            ups.append(moved[1])
            downs.append(moved[2])
    return [own] + ups[1:] + downs[1:] + far, made


def owner_place(slot, capacity):
    if lax.axis_size("dp") != 8:
        return jnp.zeros_like(slot), slot
    owner = slot // capacity
    me = lax.axis_index("dp")
    away = me // 2 - owner // 2
    near = jnp.where(away >= 0, away, 3 - away)
    rounds = jnp.array([[0, 1, 2, 3], [1, 0, 2, 3], [3, 2, 0, 1], [3, 2, 1, 0]], jnp.int32)
    far = 7 + rounds[me // 2][owner // 2]
    return jnp.where(((me ^ owner) & 1) == 0, near, far), slot % capacity


def collect(sources, which, row, counts):
    block = sources[0].shape[1:]
    total = sum(counts)

    def kernel(which_ref, row_ref, *refs):
        source_refs, out_refs = refs[: len(sources)], refs[len(sources) :]
        first = 0
        for out, count in zip(out_refs, counts):

            def one(k, carry, out=out, first=first):
                source_of, row_of = which_ref[first + k], row_ref[first + k]
                for u, source in enumerate(source_refs):

                    @pl.when(source_of == u)
                    def _(source=source):
                        out[k] = source[row_of]

                return carry

            lax.fori_loop(0, count, one, 0)
            first += count

    near = pl.BlockSpec(memory_space=pltpu.VMEM)
    scalars = pl.BlockSpec(memory_space=pltpu.SMEM)
    return pl.pallas_call(
        kernel,
        in_specs=[scalars, scalars] + [near] * len(sources),
        out_specs=[near] * len(counts),
        out_shape=[jax.ShapeDtypeStruct((count,) + block, sources[0].dtype) for count in counts],
        compiler_params=pltpu.CompilerParams(vmem_limit_bytes=24 << 20),
        cost_estimate=pl.CostEstimate(flops=0, bytes_accessed=2 * total * block[0] * block[1] * 2, transcendentals=0),
        name="collect",
    )(which, row, *sources)


def sum_to_owner(layers, block_of, capacity):
    starts, start = [], 0
    for layer in layers:
        starts.append(start)
        start += layer.shape[0]
    sources = list(layers) + [jnp.zeros((1,) + layers[0].shape[1:], layers[0].dtype)]
    which = sum((block_of >= at).astype(jnp.int32) for at in starts[1:] + [start])
    row = block_of - jnp.array(starts + [start], jnp.int32)[which]
    if lax.axis_size("dp") != 8:
        (placed,) = collect(sources, which, row, [block_of.shape[0]])
        return lax.psum_scatter(placed, "dp", scatter_dimension=0, tiled=True)
    me = lax.axis_index("dp")
    z = me // 2
    order = jnp.array([[3, 2, 1, 0], [3, 2, 0, 1], [0, 1, 3, 2], [0, 1, 2, 3]], jnp.int32)[z]
    units = jnp.concatenate([order * 2 + ((me & 1) ^ 1), order * 2 + (me & 1)])
    which = which.reshape(8, capacity)[units].reshape(-1)
    row = row.reshape(8, capacity)[units].reshape(-1)
    give = collect(sources, which[: 4 * capacity], row[: 4 * capacity], [capacity] * 4)
    keep = collect(sources, which[4 * capacity :], row[4 * capacity :], [capacity] * 4)
    across = [(i, i ^ 1) for i in range(8)]

    def swapped(k):
        return shift(give[k], "dp", across)

    def total(k, other):
        return keep[k].astype(F32) + other.astype(F32)

    def send(part, other, direction, step):
        part = (part if other is None else part + other.astype(F32)).astype(BF)
        if direction > 0:
            return shift(part, "dp", [(i, i + 2) for i in range(2 * step)])
        return shift(part, "dp", [(i, i - 2) for i in range(8 - 2 * step, 8)])

    first = total(0, swapped(0))
    moved = lax.optimization_barrier((swapped(1), send(first, None, 1, 1), send(first, None, -1, 1)))
    second = total(1, moved[0])
    up = send(jnp.where(z == 0, second, first), moved[1], 1, 2)
    down = send(jnp.where(z == 3, second, first), moved[2], -1, 2)
    moved = lax.optimization_barrier((swapped(2), up, down))
    third = total(2, moved[0])
    up = send(jnp.where(z == 1, second, third), moved[1], 1, 3)
    down = send(jnp.where(z == 2, second, third), moved[2], -1, 3)
    moved = lax.optimization_barrier((swapped(3), up, down))
    return (total(3, moved[0]) + moved[1].astype(F32) + moved[2].astype(F32)).astype(BF)


UNIT_ATTENTION = ((0, 0), (0, 1), (1, 2))
UNIT_FEED = ((1, 0), (1, 3))


def rows_of(ref):
    return ref[...].reshape(-1, ref.shape[-1])


def unit_spec(unit, blocks, like):
    return pl.BlockSpec((blocks,) + like.shape[1:], lambda *i: (unit, 0, 0))


def whole(like):
    rank = len(like.shape)
    return pl.BlockSpec(like.shape, lambda *i: (0,) * rank)


def tall(like, size):
    return pl.BlockSpec((size, like.shape[1]), lambda i: (i, 0))


def call(kernel, grid, ins, in_specs, outs, out_specs, flops, limit, scratch=(), name=None):
    moved = sum(math.prod(v.shape) * v.dtype.itemsize for v in list(ins) + list(outs))
    return pl.pallas_call(
        kernel,
        grid=grid,
        in_specs=in_specs,
        out_specs=out_specs,
        out_shape=outs,
        scratch_shapes=list(scratch),
        compiler_params=pltpu.CompilerParams(vmem_limit_bytes=limit << 20),
        cost_estimate=pl.CostEstimate(flops=int(flops), bytes_accessed=int(moved), transcendentals=0),
        name=name,
    )(*ins)


def row_block(count):
    return count // 2 if count % 32 == 0 else count


def pair_of(mine_ref, away_ref, group, value):
    wide = mine_ref.shape[2] // 2
    at = value * wide
    return jnp.concatenate([mine_ref[group, :, at : at + wide], away_ref[1 - group, :, at : at + wide]], axis=0)


def attend_kernel(
    size, causal, rows_ref, pair_ref, away_ref, own_ref, other_ref, mask_ref, place_ref,
    part_ref, e_ref, inverse_ref, mixed_ref, q_ref,
):
    wide = q_ref.shape[1] // 2
    heads = wide // size
    rows = rows_ref[...]
    count = rows.shape[0]
    lanes = lax.broadcasted_iota(jnp.int32, (count, wide), 1)
    if causal:
        allowed = place_ref[...] < mask_ref[...]
    else:
        one = (lanes == 0).astype(BF)
    ones = jnp.ones((pair_ref.shape[1] * 2, wide), BF)
    inverses = jnp.zeros((count, wide), F32)
    part = None
    for group, w_ref in enumerate((own_ref, other_ref)):
        weight = rows_of(w_ref)
        query = mm(rows, weight[:wide], NT).astype(BF)
        q_ref[:, group * wide : group * wide + wide] = query
        query = query.astype(F32) * size ** (-0.5)
        key = pair_of(pair_ref, away_ref, group, 0)
        if not causal:
            key = jnp.concatenate([key, mask_ref[...]], axis=1)
        value = jnp.concatenate([pair_of(pair_ref, away_ref, group, 1), ones], axis=1)
        mixed = None
        for h in range(heads):
            here = (lanes >= h * size) & (lanes < h * size + size)
            lhs = jnp.where(here, query, 0.0).astype(BF)
            if causal:
                scores = jnp.where(allowed, mm(lhs, key, NT), -1e30)
            else:
                scores = mm(jnp.concatenate([lhs, one], axis=1), key, NT)
            powers = jnp.exp(scores - jnp.max(scores, axis=1, keepdims=True)).astype(BF)
            e_ref[group * heads + h] = powers
            got = mm(powers, value, NN)
            inverse = 1.0 / got[:, wide:]
            inverses = jnp.where(lanes == group * heads + h, inverse, inverses)
            got = got[:, :wide] * inverse
            mixed = got if h == 0 else jnp.where(here, got, mixed)
        mixed = mixed.astype(BF)
        mixed_ref[:, group * wide : group * wide + wide] = mixed
        term = mm(mixed, weight[3 * wide :], NN)
        part = term if part is None else part + term
    inverse_ref[...] = inverses
    part_ref[...] = part.astype(BF)


def attend(rows, pair, away, weights, unit, causal, mask, place, size):
    own, other, blocks = weights
    count, width = rows.shape
    wide = pair.shape[2] // 2
    step = row_block(count)
    heads = 2 * wide // size
    spec = unit_spec(unit, blocks, own)
    sd = jax.ShapeDtypeStruct
    return call(
        functools.partial(attend_kernel, size, causal),
        (count // step,),
        [rows, pair, away, own, other, mask, place],
        [tall(rows, step), whole(pair), whole(away), spec, spec, tall(mask, step) if causal else whole(mask), whole(place)],
        [
            sd((count, width), BF), pltpu.HBM((heads, count, 2 * count), BF), sd((count, wide), F32),
            sd((count, 2 * wide), BF), sd((count, 2 * wide), BF),
        ],
        [
            pl.BlockSpec((step, width), lambda i: (i, 0)),
            pl.BlockSpec((heads, step, 2 * count), lambda i: (0, i, 0)),
            pl.BlockSpec((step, wide), lambda i: (i, 0)),
            pl.BlockSpec((step, 2 * wide), lambda i: (i, 0)),
            pl.BlockSpec((step, 2 * wide), lambda i: (i, 0)),
        ],
        16 * heads * count * count * size,
        32,
        name="attend",
    )


def attend_back_kernel(
    size, g_ref, e_ref, inverse_ref, mixed_ref, q_ref, pair_ref, away_ref, own_ref, other_ref,
    dq_ref, rows_ref, mine_ref, give_ref, total,
):
    step = pl.program_id(0)
    wide = q_ref.shape[1] // 2
    heads = wide // size
    count = pair_ref.shape[1]
    scale = size ** (-0.5)
    lanes = lax.broadcasted_iota(jnp.int32, (q_ref.shape[0], wide), 1)
    grad = g_ref[...]

    @pl.when(step == 0)
    def _():
        total[...] = jnp.zeros_like(total)

    rows = None
    for group, w_ref in enumerate((own_ref, other_ref)):
        weight = rows_of(w_ref)
        cols = slice(group * wide, group * wide + wide)
        key = pair_of(pair_ref, away_ref, group, 0)
        value = pair_of(pair_ref, away_ref, group, 1)
        back = mm(grad, weight[3 * wide :], NT).astype(BF).astype(F32)
        inner = back * mixed_ref[:, cols].astype(F32)
        inverses = [inverse_ref[:, group * heads + h : group * heads + h + 1] for h in range(heads)]
        spread = jnp.broadcast_to(inverses[0], back.shape)
        for h in range(1, heads):
            spread = jnp.where(lanes >= h * size, inverses[h], spread)
        back = back * spread
        inner = inner * spread
        back_t = back.T.astype(BF)
        query_t = (q_ref[:, cols].astype(F32) * scale).T.astype(BF)
        dq = None
        for h in range(heads):
            here = (lanes >= h * size) & (lanes < h * size + size)
            powers = e_ref[group * heads + h]
            level = jnp.sum(jnp.where(here, inner, 0.0), axis=1, keepdims=True)
            slope = mm(jnp.where(here, back, 0.0).astype(BF), value, NT)
            ds = (powers.astype(F32) * (slope - level)).astype(BF)
            got = mm(ds, key, NN)
            dq = got if h == 0 else jnp.where(here, got, dq)
            k_at = group * 2 * wide + h * size
            v_at = k_at + wide
            total[k_at : k_at + size, :] += mm(query_t[h * size : h * size + size], ds, NN)
            total[v_at : v_at + size, :] += mm(back_t[h * size : h * size + size], powers, NN)
        dq = (dq * scale).astype(BF)
        dq_ref[:, cols] = dq
        term = mm(dq, weight[:wide], NN)
        rows = term if rows is None else rows + term
    rows_ref[...] = rows.astype(rows_ref.dtype)

    @pl.when(step == pl.num_programs(0) - 1)
    def _():
        mine_ref[...] = total[:, :count]
        give_ref[: 2 * wide, :] = total[2 * wide :, count:].astype(BF)
        give_ref[2 * wide :, :] = total[: 2 * wide, count:].astype(BF)


def attend_back(grad, powers, inverse, mixed, query, pair, away, weights, unit, size, kind):
    own, other, blocks = weights
    count, width = grad.shape
    wide = inverse.shape[1]
    step = row_block(count)
    heads = 2 * wide // size
    spec = unit_spec(unit, blocks, own)
    sd = jax.ShapeDtypeStruct
    flat = sd((4 * wide, count), F32)
    return call(
        functools.partial(attend_back_kernel, size),
        (count // step,),
        [grad, powers, inverse, mixed, query, pair, away, own, other],
        [
            tall(grad, step), pl.BlockSpec((heads, step, 2 * count), lambda i: (0, i, 0)), tall(inverse, step),
            tall(mixed, step), tall(query, step), whole(pair), whole(away), spec, spec,
        ],
        [sd((count, 2 * wide), BF), sd((count, width), kind), flat, sd(flat.shape, BF)],
        [
            pl.BlockSpec((step, 2 * wide), lambda i: (i, 0)),
            pl.BlockSpec((step, width), lambda i: (i, 0)),
            whole(flat),
            whole(flat),
        ],
        32 * heads * count * count * size,
        32,
        scratch=[pltpu.VMEM((4 * wide, 2 * count), F32)],
        name="attend_back",
    )


def feed_kernel(rows_ref, own_in, other_in, own_out, other_out, part_ref, active_ref, slope_ref):
    rows = rows_ref[...]
    size = active_ref.shape[1] // 2
    part = None
    for group, (w_in, w_out) in enumerate(((own_in, own_out), (other_in, other_out))):
        u = mm(rows, rows_of(w_in), NT)
        phi = 0.5 + 0.5 * lax.erf(u * 0.5**0.5)
        active = (u * phi).astype(BF)
        active_ref[:, group * size : group * size + size] = active
        slope_ref[:, group * size : group * size + size] = (
            phi + u * (jnp.exp(-0.5 * u * u) * 0.3989422804014327)
        ).astype(BF)
        term = mm(active, rows_of(w_out), NN)
        part = term if part is None else part + term
    part_ref[...] = part.astype(BF)


def feed(rows, weights, unit):
    own, other, blocks = weights
    count, width = rows.shape
    step = row_block(count)
    size = 2 * blocks * own.shape[1]
    first, second = unit_spec(unit, blocks, own), unit_spec(unit + 1, blocks, own)
    sd = jax.ShapeDtypeStruct
    return call(
        feed_kernel, (count // step,), [rows, own, other, own, other], [tall(rows, step), first, first, second, second],
        [sd((count, width), BF), sd((count, size), BF), sd((count, size), BF)],
        [pl.BlockSpec((step, w), lambda i: (i, 0)) for w in (width, size, size)],
        4 * count * width * size,
        20,
        name="feed",
    )


def per_device(
    source,
    target,
    out_grad,
    src_len,
    tgt_len,
    owners,
    master,
    rotated_first_moment,
    rotated_second_moment,
    stat_left,
    stat_right,
    basis_left,
    basis_right,
    norm_params,
    norm_one,
    norm_two,
):
    tensor_count = lax.axis_size("tensor")
    me = lax.axis_index("tensor")
    core = me & 1
    head_count = HEADS // tensor_count
    col_count = FFB // tensor_count
    capacity = master.shape[1]
    slot_count = capacity * lax.axis_size("dp")
    row_count = source.shape[1]
    block_rows = master.shape[2]
    width = master.shape[3]

    half = max(capacity // 2, 1)
    sources, made = gather_owners(
        master[0].astype(BF),
        [
            lambda: (before(stat_right[0], basis_right[0], 0, half), gather_chips(source[0])),
            lambda: (before(stat_right[0], basis_right[0], half, capacity - half), gather_chips(target[0])),
            lambda: gather_chips(out_grad[0]),
        ],
    )
    (early, src), (late, tgt), cot = made
    slot_of = slot_positions(owners[0], capacity)
    which, row = owner_place(slot_of, capacity)
    order = [j for unit in (0, 3, 1, 2, 4, 5, 6) for j in range(unit * col_count, (unit + 1) * col_count)]
    order = jnp.array(order, jnp.int32)
    blocks = collect(sources, which[order], row[order], [2 * col_count, 5 * col_count])
    weights = [(part, swap_core(part), col_count) for part in blocks]
    wide = head_count * block_rows

    chips = tensor_count // 2
    local = lax.iota(jnp.int32, row_count * chips)
    own_pos = (local // row_count) * (2 * row_count) + core * row_count + local % row_count
    other_pos = own_pos + (1 - 2 * core) * row_count
    key_pos = jnp.concatenate([own_pos, other_pos])
    gains = norm_params[0]
    shifts = norm_params[1]
    src_size = src_len[0]
    tgt_size = tgt_len[0]
    total_rows = local.shape[0]
    place = key_pos[None, :]
    first_lane = lax.iota(jnp.int32, wide)[None, :] == 0
    enc_mask = jnp.where((key_pos[:, None] >= src_size) & first_lane, -1e30, 0.0).astype(BF)
    dec_mask = jnp.minimum(own_pos + 1, tgt_size)[:, None]
    keep_rows = (own_pos < tgt_size).astype(F32)[:, None]

    def matrices(place_of, start, stop):
        part, unit = place_of
        at = unit * col_count
        return [w[at + start : at + stop].reshape(-1, width) for w in weights[part][:2]]

    def attention(query_rows, key_rows, unit, causal):
        pair = jnp.stack([mm(key_rows, w, NT).astype(BF) for w in matrices(unit, head_count, 3 * head_count)])
        away = swap_core(pair)
        mask = dec_mask if causal else enc_mask
        part, *saved = attend(query_rows, pair, away, weights[unit[0]], unit[1], causal, mask, place, block_rows)
        return part, saved + [pair, away]

    def halves(first, second):
        half = first.shape[1] // 2
        return mm(first[:, :half], second, TN), mm(first[:, half:], second, TN)

    def attention_back(grad, saved, query_rows, key_rows, unit, together):
        powers, inverse, mixed, query, pair, away = saved
        grad_b = grad.astype(BF)
        dq, query_part, mine, give = attend_back(
            grad_b, powers, inverse, mixed, query, pair, away, weights[unit[0]], unit[1], block_rows, F32 if together else BF
        )
        both = (mine + swap_core(give).astype(F32)).astype(BF)
        parts = [both[: 2 * wide], both[2 * wide :]]
        key_part = sum(mm(p, w, TN) for p, w in zip(parts, matrices(unit, head_count, 3 * head_count)))
        if together:
            key_part = key_part + query_part
        grad_q = halves(dq, query_rows)
        grad_o = halves(mixed, grad_b)
        grads = [[grad_q[at], mm(parts[at], key_rows, NN), grad_o[at]] for at in range(2)]
        return grads, query_part, key_part

    def feeding(rows, unit):
        part, active, slope = feed(rows, weights[unit[0]], unit[1])
        return part, (active, slope)

    def feeding_back(grad, saved, rows, unit):
        active, slope = saved
        grad_b = grad.astype(BF)
        half = active.shape[1] // 2
        grads, part = [], 0.0
        for at, w_in, w_out in zip(range(2), matrices(unit, 0, col_count), matrices((unit[0], unit[1] + 1), 0, col_count)):
            cols = slice(at * half, at * half + half)
            du = (mm(grad_b, w_out, NT) * slope[:, cols].astype(F32)).astype(BF)
            part = part + mm(du, w_in, NN)
            grads.append([mm(du, rows, TN), mm(active[:, cols], grad_b, TN)])
        return grads, part

    one, three, four = UNIT_ATTENTION
    two, five = UNIT_FEED
    branch_one, saved_one = attention(src, src, one, False)
    z_one = src.astype(F32) + sum_chips(branch_one)
    h_one, pull_one = jax.vjp(layer_norm, z_one, gains[0], shifts[0])
    h_one_b = h_one.astype(BF)
    branch_two, saved_two = feeding(h_one_b, two)
    z_two = h_one + sum_chips(branch_two)
    encoded, pull_two = jax.vjp(layer_norm, z_two, gains[1], shifts[1])
    encoded_b = encoded.astype(BF)
    branch_three, saved_three = attention(tgt, tgt, three, True)
    z_three = tgt.astype(F32) + sum_chips(branch_three)
    g_one, pull_three = jax.vjp(layer_norm, z_three, gains[2], shifts[2])
    g_one_b = g_one.astype(BF)
    branch_four, saved_four = attention(g_one_b, encoded_b, four, False)
    z_four = g_one + sum_chips(branch_four)
    g_two, pull_four = jax.vjp(layer_norm, z_four, gains[3], shifts[3])
    g_two_b = g_two.astype(BF)
    branch_five, saved_five = feeding(g_two_b, five)
    z_five = g_two + sum_chips(branch_five)
    normed, pull_five = jax.vjp(layer_norm, z_five, gains[4], shifts[4])
    decoded = own_rows((normed * keep_rows).astype(BF))

    grad_z_five, gain_five, shift_five = pull_five(cot.astype(F32) * keep_rows)
    weights_five, rows_five = feeding_back(grad_z_five, saved_five, g_two_b, five)
    grad_z_four, gain_four, shift_four = pull_four(grad_z_five + sum_chips(rows_five))
    weights_four, query_four, key_four = attention_back(grad_z_four, saved_four, g_one_b, encoded_b, four, False)
    grad_encoded = sum_chips(key_four)
    query_four, weights_four = lax.optimization_barrier((query_four, weights_four))
    query_sum = sum_chips(query_four)
    grad_z_two, gain_two, shift_two = pull_two(grad_encoded)
    weights_two, rows_two = feeding_back(grad_z_two, saved_two, h_one_b, two)
    query_sum, rows_two = lax.optimization_barrier((query_sum, rows_two.astype(BF)))
    sum_two = sum_chips(rows_two)
    grad_z_three, gain_three, shift_three = pull_three(grad_z_four + query_sum)
    weights_three, _, rows_three = attention_back(grad_z_three, saved_three, tgt, tgt, three, True)
    sum_two, rows_three = lax.optimization_barrier((sum_two, rows_three))
    tgt_grad = own_rows(grad_z_three) + sum_chips_own(rows_three)
    grad_z_one, gain_one, shift_one = pull_one(grad_z_two + sum_two)
    weights_one, _, rows_one = attention_back(grad_z_one, saved_one, src, src, one, True)
    src_grad = own_rows(grad_z_one) + sum_chips_own(rows_one)

    def reduce_core(grads):
        mine, give = [jnp.concatenate(part, axis=0) for part in grads]
        total = mine + swap_core(give.astype(BF)).astype(F32)
        return total.astype(BF).reshape(-1, block_rows, width)

    layers = [reduce_core(item) for item in (weights_one, weights_two, weights_three, weights_four, weights_five)]
    norm_local = jnp.stack(
        [
            jnp.stack([gain_one, gain_two, gain_three, gain_four, gain_five]),
            jnp.stack([shift_one, shift_two, shift_three, shift_four, shift_five]),
        ]
    )
    held = slot_of[None, :] == jnp.arange(slot_count, dtype=jnp.int32)[:, None]
    block_of = jnp.sum(jnp.where(held, jnp.arange(slot_of.shape[0], dtype=jnp.int32)[None, :], 0), axis=1)
    block_of = jnp.where(jnp.any(held, axis=1), block_of, slot_of.shape[0])
    own_grad = sum_to_owner(layers, block_of, capacity)
    norm_grad = sum_everywhere(norm_local)
    results = after(
        own_grad,
        master[0],
        rotated_first_moment[0],
        rotated_second_moment[0],
        stat_left[0],
        basis_left[0],
        stat_right[0],
        basis_right[0],
        early,
        late,
    )
    norm_one_new = 0.9 * norm_one + 0.1 * norm_grad
    norm_two_new = 0.999 * norm_two + 0.001 * norm_grad * norm_grad
    norm_new = norm_params - rate_vector * (norm_one_new / FIX_ONE) / (jnp.sqrt(norm_two_new / FIX_TWO) + 1e-08)
    return (
        decoded[None],
        src_grad[None],
        tgt_grad[None],
        results[0][None],
        results[1][None],
        results[2][None],
        results[3][None],
        results[4][None],
        results[5][None],
        results[6][None],
        results[7][None],
        norm_new,
        norm_one_new,
        norm_two_new,
    )


def solution(mesh):
    in_specs = (
        P("dp", "tensor", None),
        P("dp", "tensor", None),
        P("dp", "tensor", None),
        P("dp"),
        P("dp"),
        P("tensor", None),
        P("tensor", "dp", None, None),
        P("tensor", "dp", None, None),
        P("tensor", "dp", None, None),
        P("tensor", "dp", None, None),
        P("tensor", "dp", None, None),
        P("tensor", "dp", None, None),
        P("tensor", "dp", None, None),
        P(),
        P(),
        P(),
    )
    out_specs = (
        P("dp", "tensor", None),
        P("dp", "tensor", None),
        P("dp", "tensor", None),
        P("tensor", "dp", None, None),
        P("tensor", "dp", None, None),
        P("tensor", "dp", None, None),
        P("tensor", "dp", None, None),
        P("tensor", "dp", None, None),
        P("tensor", "dp", None, None),
        P("tensor", "dp", None, None),
        P("tensor", "dp", None, None),
        P(),
        P(),
        P(),
    )
    return jax.shard_map(
        per_device, mesh=mesh, in_specs=in_specs, out_specs=out_specs, check_vma=False
    )
```

```python
import functools
import math

import jax
import jax.numpy as jnp
from jax import lax
from jax.experimental import pallas as pl
from jax.experimental.pallas import tpu as pltpu
from jax.sharding import PartitionSpec as P

HEADS = 8
STEP = 10
FFB = 32


highest = lax.Precision.HIGHEST
rate_matrix = 0.3
rate_vector = 0.6


def slot_positions(owner_row, capacity):
    block_ids = jnp.arange(owner_row.shape[0], dtype=jnp.int32)
    same_owner = (owner_row[:, None] == owner_row[None, :]).astype(jnp.int32)
    earlier = (block_ids[None, :] < block_ids[:, None]).astype(jnp.int32)
    rank_of = jnp.sum(same_owner * earlier, axis=1)
    return owner_row * capacity + rank_of


def layer_norm(values, norm_gain, norm_shift):
    center = values - jnp.mean(values, axis=-1, keepdims=True)
    spread = jnp.mean(center * center, axis=-1, keepdims=True)
    return center * lax.rsqrt(spread + 1e-05) * norm_gain + norm_shift


F32 = jnp.float32
BF = jnp.bfloat16
NN = (((1,), (0,)), ((), ()))
NT = (((1,), (1,)), ((), ()))
TN = (((0,), (0,)), ((), ()))
FIX_ONE = 1.0 - 0.9**STEP
FIX_TWO = 1.0 - 0.999**STEP


def split(v):
    hi = v.astype(BF)
    return hi, (v - hi.astype(F32)).astype(BF)


def mm(a, b, dims):
    return lax.dot_general(a, b, dims, preferred_element_type=F32)


def mm3(a, b, dims):
    ah, al = a if isinstance(a, tuple) else split(a)
    bh, bl = b if isinstance(b, tuple) else split(b)
    return mm(ah, bh, dims) + (mm(ah, bl, dims) + mm(al, bh, dims))


def before_kernel(s_ref, q_ref, a_ref, m_ref):
    half = s_ref.shape[1] // 2
    q = split(q_ref[0])
    a = 0.95 * mm3(s_ref[0], q, NN)
    a_ref[0] = a
    ah, al = split(a)
    m_ref[0, :half, :] = mm3((ah[:, :half], al[:, :half]), (ah, al), TN)
    m_ref[0, half:, half:] = mm3((ah[:, half:], al[:, half:]), (ah[:, half:], al[:, half:]), TN)


def before(stat, basis, start, n):
    w = stat.shape[1]
    take = pl.BlockSpec((1, w, w), lambda i: (i + start, 0, 0))
    spec = pl.BlockSpec((1, w, w), lambda i: (i, 0, 0))
    return pl.pallas_call(
        before_kernel,
        grid=(n,),
        in_specs=[take, take],
        out_specs=[spec, spec],
        out_shape=[pltpu.HBM((n, w, w), F32)] * 2,
        compiler_params=pltpu.CompilerParams(vmem_limit_bytes=24 << 20),
        cost_estimate=pl.CostEstimate(flops=n * 12 * w**3, bytes_accessed=n * 16 * w * w, transcendentals=0),
        name="before",
    )(pltpu.with_memory_space_constraint(stat, pltpu.HBM), pltpu.with_memory_space_constraint(basis, pltpu.HBM))


PANEL = 16
BLOCK = 128


def reciprocal(v):
    guess = pl.reciprocal(v, approx=True)
    for _ in range(2):
        guess = guess * (2.0 - v * guess)
    return guess


def factor_panels(dm, dw, pm, pw, um, uw, n, panels):
    size = BLOCK
    end = panels * PANEL
    for s in range(n):
        pm[s * PANEL : s * PANEL + PANEL, :] = dm[s * size : s * size + PANEL, :]
        pw[s * PANEL : s * PANEL + PANEL, :] = dw[s * size : s * size + PANEL, :]
    for p in range(panels):
        top = p * PANEL
        low = top + PANEL
        rows = [pm[pl.ds(a, n, stride=PANEL), :] for a in range(PANEL)]
        eyes = [pw[pl.ds(a, n, stride=PANEL), :] for a in range(PANEL)]
        corner = {}
        for a in range(PANEL):
            for b in range(a, PANEL):
                corner[a, b] = jnp.broadcast_to(rows[a][:, top + b : top + b + 1], (n, size))
        for r in range(PANEL):
            inverse = reciprocal(corner[r, r])
            for a in range(r + 1, PANEL):
                factor = corner[r, a] * inverse
                for b in range(a, PANEL):
                    corner[a, b] = corner[a, b] - factor * corner[r, b]
                rows[a] = rows[a] - factor * rows[r]
                eyes[a] = eyes[a] - factor * eyes[r]
            scale = lax.rsqrt(corner[r, r])
            um[pl.ds(r, n, stride=PANEL), :] = rows[r] * scale
            uw[pl.ds(r, n, stride=PANEL), :] = eyes[r] * scale
        pending = []
        for s in range(n):
            base = s * size
            upper = um[s * PANEL : s * PANEL + PANEL, :]
            lower = uw[s * PANEL : s * PANEL + PANEL, :]
            dw[base + top : base + low, :] = lower
            if low < end:
                uh, ul = split(upper)
                lh, ll = split(lower)
                lhs = jnp.concatenate([uh, uh, ul], axis=0)
                high = jnp.concatenate([uh, lh], axis=1)
                rest = jnp.concatenate([ul, ll], axis=1)
                rhs = jnp.concatenate([high, rest, high], axis=0)
                u = mm(lhs[:, low : low + PANEL], rhs, TN)
                pm[s * PANEL : s * PANEL + PANEL, :] = dm[base + low : base + low + PANEL, :] - u[:, :size]
                pw[s * PANEL : s * PANEL + PANEL, :] = dw[base + low : base + low + PANEL, :] - u[:, size:]
                if low + PANEL < end:
                    pending.append((base, lhs, rhs))
        for base, lhs, rhs in pending:
            u = mm(lhs[:, low + PANEL : end], rhs, TN)
            lo, hi = base + low + PANEL, base + end
            dm[lo:hi, :] = dm[lo:hi, :] - u[:, :size]
            dw[lo:hi, :] = dw[lo:hi, :] - u[:, size:]


def after_kernel(
    g_ref, w_ref, m1_ref, m2_ref, l_ref, ql_ref, s_ref, q_ref, ae_ref, me_ref, al_ref, ml_ref,
    w_out, m1_out, m2_out, l_out, s_out, qln_out, q_out, c_out,
    gram, gram_left, x_left, dm, dw, pm, pw, um, uw,
):
    step = pl.program_id(0)
    count = pl.num_programs(0)
    n = q_out.shape[0]
    width = g_ref.shape[2]
    rows = g_ref.shape[1]
    per = g_ref.shape[0]
    blk = BLOCK

    def one_slot(i, a_ref, m_ref):
        slot = step * per + i
        g = g_ref[i]
        q = split(q_ref[i])
        ql = split(ql_ref[i])
        p = mm(g, q[0], NN) + mm(g, q[1], NN)
        k = mm(g, g, NT)
        a = a_ref[i]
        a_parts = split(a)
        b = 0.05 * p
        bh, bl = split(b)
        h = mm(g, a_parts[0], NN) + mm(g, a_parts[1], NN) + 0.5 * mm3(k, (bh, bl), NN)
        q_out[slot] = a + mm(jnp.concatenate([g, g], axis=0), jnp.concatenate([bh, bl], axis=0), TN)
        hh, hl = split(h)
        y = jnp.concatenate([hh, bh, hh, bh, hl, bl], axis=0)
        z = jnp.concatenate([bh, hh, bl, hl, bh, hh], axis=0)
        for j in range(width // blk):
            lo = j * blk
            gram[slot, lo : lo + blk, lo:] = m_ref[i, lo : lo + blk, lo:] + mm(y[:, lo : lo + blk], z[:, lo:], TN)
        left = 0.95 * l_ref[i] + 0.05 * k
        l_out[i] = left
        xl = mm3(left, ql, NN)
        x_left[slot] = xl
        gram_left[slot] = mm3(xl, xl, TN)
        s_out[i] = 0.95 * s_ref[i] + 0.05 * mm(g, g, TN)
        turned = mm3(ql, p, TN)
        first = 0.9 * m1_ref[i] + 0.1 * turned
        second = 0.999 * m2_ref[i] + 0.001 * turned * turned
        m1_out[i] = first
        m2_out[i] = second
        direction = first / FIX_ONE / (jnp.sqrt(second / FIX_TWO) + 1e-08)
        update = mm3(ql, mm3(direction, q, NT), NN)
        weight = w_ref[i]
        weight = weight - rate_matrix * (update + 0.01 * weight)
        w_out[i] = weight
        c_out[i] = weight.astype(BF)

    @pl.when(step * per < n // 2)
    def _():
        for i in range(per):
            one_slot(i, ae_ref, me_ref)

    @pl.when(step * per >= n // 2)
    def _():
        for i in range(per):
            one_slot(i, al_ref, ml_ref)

    @pl.when(step == count - 1)
    def _():
        eye = (lax.broadcasted_iota(jnp.int32, (blk, blk), 0) == lax.broadcasted_iota(jnp.int32, (blk, blk), 1)).astype(F32)
        blocks = width // blk

        def at(s):
            return slice(s * blk, s * blk + blk)

        for s in range(n):
            dm[at(s), :] = eye
            dm[s * blk : s * blk + rows, :rows] = gram_left[s]
            dw[at(s), :] = eye
        factor_panels(dm, dw, pm, pw, um, uw, n, rows // PANEL)
        for s in range(n):
            qln_out[s] = mm3(x_left[s], dw[s * blk : s * blk + rows, :rows], NT)

        def block_step(kk, carry):
            for kb in range(blocks):
                @pl.when(kk == kb)
                def _():
                    for s in range(n):
                        dm[at(s), :] = gram[s, kb * blk : kb * blk + blk, kb * blk : kb * blk + blk]
            for s in range(n):
                dw[at(s), :] = eye
            factor_panels(dm, dw, pm, pw, um, uw, n, blk // PANEL)

            for kb in range(blocks):
                @pl.when(kk == kb)
                def _():
                    lo = kb * blk
                    hi = lo + blk

                    def one(s, c):
                        inv = dw[pl.ds(pl.multiple_of(s * blk, blk), blk), :]
                        gram[s, lo:hi, lo:hi] = inv
                        if blocks == 1:
                            return c
                        ih, il = split(inv)
                        lhs = jnp.concatenate([ih, ih, il], axis=1)

                        def scaled(part):
                            ph, plo = split(part)
                            return mm(lhs, jnp.concatenate([ph, plo, ph], axis=0), NN)

                        if kb > 0:
                            gram[s, lo:hi, :lo] = scaled(gram[s, lo:hi, :lo])
                        if hi < width:
                            up = scaled(gram[s, lo:hi, hi:])
                            uh, ul = split(up)
                            rh, rl = split(gram[s, lo:hi, :hi])
                            us = jnp.concatenate([uh, uh, ul], axis=0)
                            vs = jnp.concatenate([uh, ul, uh], axis=0)
                            rs = jnp.concatenate([rh, rl, rh], axis=0)
                            below = mm(us, rs, TN)
                            if kb > 0:
                                gram[s, hi:, :lo] = gram[s, hi:, :lo] - below[:, :lo]
                            gram[s, hi:, lo:hi] = -below[:, lo:]
                            for i in range(kb + 1, blocks):
                                b0 = i * blk
                                gram[s, b0 : b0 + blk, b0:] = gram[s, b0 : b0 + blk, b0:] - mm(
                                    us[:, b0 - hi : b0 - hi + blk], vs[:, b0 - hi :], TN
                                )
                        return c

                    lax.fori_loop(0, n, one, 0, unroll=min(n, 4))
            return carry

        lax.fori_loop(0, blocks, block_step, 0)

        def finish(s, c):
            x = split(q_out[s])
            for i in range(0, width, 2 * blk):
                hi = i + 2 * blk
                zz = gram[s, i:hi, :hi]
                r_i = lax.broadcasted_iota(jnp.int32, (2 * blk, hi), 0) + i
                c_i = lax.broadcasted_iota(jnp.int32, (2 * blk, hi), 1)
                zz = jnp.where(c_i <= r_i, zz, 0.0)
                q_out[s, :, i:hi] = mm3((x[0][:, :hi], x[1][:, :hi]), zz, NT)
            return c

        lax.fori_loop(0, n, finish, 0, unroll=min(n, 2))


def after(grad, weight, m1, m2, left, ql, stat, q, early, late):
    n, rows, width = weight.shape
    per = 2 if n % 4 == 0 else 1
    half = n // 2 // per
    first = pl.BlockSpec((per, width, width), lambda i: (jnp.minimum(i, half - 1), 0, 0))
    second = pl.BlockSpec((per, width, width), lambda i: (jnp.maximum(i - half, 0), 0, 0))
    wide = pl.BlockSpec((per, width, width), lambda i: (i, 0, 0))
    flat = pl.BlockSpec((per, rows, width), lambda i: (i, 0, 0))
    small = pl.BlockSpec((per, rows, rows), lambda i: (i, 0, 0))
    sd = jax.ShapeDtypeStruct
    return pl.pallas_call(
        after_kernel,
        grid=(n // per,),
        in_specs=[flat, flat, flat, flat, small, small, wide, wide, first, first, second, second],
        out_specs=[
            flat, flat, flat, small, wide,
            pl.BlockSpec((n, rows, rows), lambda i: (0, 0, 0)),
            pl.BlockSpec((n, width, width), lambda i: (0, 0, 0)),
            flat,
        ],
        out_shape=[
            sd(weight.shape, F32), sd(weight.shape, F32), sd(weight.shape, F32), sd(left.shape, F32), sd(stat.shape, F32),
            sd(ql.shape, F32), sd(q.shape, F32), sd(weight.shape, BF),
        ],
        scratch_shapes=[
            pltpu.VMEM((n, width, width), F32),
            pltpu.VMEM((n, rows, rows), F32),
            pltpu.VMEM((n, rows, rows), F32),
            pltpu.VMEM((n * BLOCK, BLOCK), F32),
            pltpu.VMEM((n * BLOCK, BLOCK), F32),
            pltpu.VMEM((n * PANEL, BLOCK), F32),
            pltpu.VMEM((n * PANEL, BLOCK), F32),
            pltpu.VMEM((n * PANEL, BLOCK), F32),
            pltpu.VMEM((n * PANEL, BLOCK), F32),
        ],
        compiler_params=pltpu.CompilerParams(vmem_limit_bytes=62 << 20),
        cost_estimate=pl.CostEstimate(flops=n * 12 * width**3, bytes_accessed=n * 24 * width * width, transcendentals=0),
        name="after",
    )(grad, weight, m1, m2, left, ql, stat, q, *early, *late)


def swap_core(values):
    count = lax.axis_size("tensor")
    return lax.ppermute(values, "tensor", [(i, i ^ 1) for i in range(count)])


def chip_bits():
    bit, bits = 2, []
    while bit < lax.axis_size("tensor"):
        bits.append(bit)
        bit *= 2
    return bits


def swap_chip(values, bit):
    count = lax.axis_size("tensor")
    return lax.ppermute(values, "tensor", [(i, i ^ bit) for i in range(count)])


def gather_chips(rows):
    for bit in chip_bits():
        other = swap_chip(rows, bit)
        upper = (lax.axis_index("tensor") & bit) != 0
        rows = jnp.where(
            upper, jnp.concatenate([other, rows], axis=0), jnp.concatenate([rows, other], axis=0)
        )
    return rows


def sum_chips(part):
    for bit in chip_bits():
        part = part.astype(BF)
        part = part.astype(F32) + swap_chip(part, bit).astype(F32)
    return part.astype(F32)


def other_chips(part):
    part, got = part.astype(BF), None
    for bit in chip_bits():
        moved = swap_chip(part, bit).astype(F32)
        got = moved if got is None else got + moved
        part = part if bit == chip_bits()[-1] else (part.astype(F32) + moved).astype(BF)
    return jnp.zeros(part.shape, F32) if got is None else got


def own_rows(values):
    chips = lax.axis_size("tensor") // 2
    count = values.shape[0] // chips
    return lax.dynamic_slice_in_dim(values, (lax.axis_index("tensor") // 2) * count, count, 0)


def sum_chips_own(part):
    for bit in reversed(chip_bits()):
        half = part.shape[0] // 2
        upper = (lax.axis_index("tensor") & bit) != 0
        keep = jnp.where(upper, part[half:], part[:half])
        give = jnp.where(upper, part[:half], part[half:]).astype(BF)
        part = keep.astype(F32) + swap_chip(give, bit).astype(F32)
    return part


def sum_everywhere(values):
    values = values + swap_core(values)
    count = lax.axis_size("dp")
    if count & (count - 1):
        return lax.psum(values, "dp")
    bit = 1
    while bit < count:
        values = values + lax.ppermute(values, "dp", [(i, i ^ bit) for i in range(count)])
        bit *= 2
    return values


def shift(values, axis, pairs):
    return lax.ppermute(values, axis, pairs)


def gather_owners(own, beside):
    count = lax.axis_size("dp")
    if count != 8:
        return [lax.all_gather(own, "dp", axis=0, tiled=True)], [make() for make in beside]
    across = [(i, i ^ 1) for i in range(8)]
    z = lax.axis_index("dp") // 2
    even = (z & 1) == 0
    ups, downs, far = [own], [own], []
    made = []
    for s in range(4):
        if s == 0:
            pay = own
        elif s == 1:
            pay = jnp.where(even, downs[1], ups[1])
        elif s == 2:
            pay = jnp.where(z == 0, downs[2], jnp.where(z == 1, downs[1], jnp.where(z == 2, ups[1], ups[2])))
        else:
            pay = jnp.where(z == 0, downs[3], jnp.where(z == 1, downs[2], jnp.where(z == 2, ups[2], ups[3])))
        moved = [shift(pay, "dp", across)]
        if s < 3:
            moved.append(shift(ups[s], "dp", [(i, i + 2) for i in range(2 * s, 6)]))
            moved.append(shift(downs[s], "dp", [(i, i - 2) for i in range(2, 8 - 2 * s)]))
        extra = [beside[s]()] if s < len(beside) else []
        moved, extra = lax.optimization_barrier((moved, extra))
        made.extend(extra)
        far.append(moved[0])
        if s < 3:
            ups.append(moved[1])
            downs.append(moved[2])
    return [own] + ups[1:] + downs[1:] + far, made


def owner_place(slot, capacity):
    if lax.axis_size("dp") != 8:
        return jnp.zeros_like(slot), slot
    owner = slot // capacity
    me = lax.axis_index("dp")
    away = me // 2 - owner // 2
    near = jnp.where(away >= 0, away, 3 - away)
    rounds = jnp.array([[0, 1, 2, 3], [1, 0, 2, 3], [3, 2, 0, 1], [3, 2, 1, 0]], jnp.int32)
    far = 7 + rounds[me // 2][owner // 2]
    return jnp.where(((me ^ owner) & 1) == 0, near, far), slot % capacity


def collect(sources, which, row, counts):
    block = sources[0].shape[1:]
    total = sum(counts)

    def kernel(which_ref, row_ref, *refs):
        source_refs, out_refs = refs[: len(sources)], refs[len(sources) :]
        first = 0
        for out, count in zip(out_refs, counts):

            def one(k, carry, out=out, first=first):
                source_of, row_of = which_ref[first + k], row_ref[first + k]
                for u, source in enumerate(source_refs):

                    @pl.when(source_of == u)
                    def _(source=source):
                        out[k] = source[row_of]

                return carry

            lax.fori_loop(0, count, one, 0)
            first += count

    near = pl.BlockSpec(memory_space=pltpu.VMEM)
    scalars = pl.BlockSpec(memory_space=pltpu.SMEM)
    return pl.pallas_call(
        kernel,
        in_specs=[scalars, scalars] + [near] * len(sources),
        out_specs=[near] * len(counts),
        out_shape=[jax.ShapeDtypeStruct((count,) + block, sources[0].dtype) for count in counts],
        compiler_params=pltpu.CompilerParams(vmem_limit_bytes=24 << 20),
        cost_estimate=pl.CostEstimate(flops=0, bytes_accessed=2 * total * block[0] * block[1] * 2, transcendentals=0),
        name="collect",
    )(which, row, *sources)


def sum_to_owner(layers, block_of, capacity):
    starts, start = [], 0
    for layer in layers:
        starts.append(start)
        start += layer.shape[0]
    sources = list(layers) + [jnp.zeros((1,) + layers[0].shape[1:], layers[0].dtype)]
    which = sum((block_of >= at).astype(jnp.int32) for at in starts[1:] + [start])
    row = block_of - jnp.array(starts + [start], jnp.int32)[which]
    if lax.axis_size("dp") != 8:
        (placed,) = collect(sources, which, row, [block_of.shape[0]])
        return lax.psum_scatter(placed, "dp", scatter_dimension=0, tiled=True)
    me = lax.axis_index("dp")
    z = me // 2
    order = jnp.array([[3, 2, 1, 0], [3, 2, 0, 1], [0, 1, 3, 2], [0, 1, 2, 3]], jnp.int32)[z]
    units = jnp.concatenate([order * 2 + ((me & 1) ^ 1), order * 2 + (me & 1)])
    which = which.reshape(8, capacity)[units].reshape(-1)
    row = row.reshape(8, capacity)[units].reshape(-1)
    give = collect(sources, which[: 4 * capacity], row[: 4 * capacity], [capacity] * 4)
    keep = collect(sources, which[4 * capacity :], row[4 * capacity :], [capacity] * 4)
    across = [(i, i ^ 1) for i in range(8)]

    def swapped(k):
        return shift(give[k], "dp", across)

    def total(k, other):
        return keep[k].astype(F32) + other.astype(F32)

    def send(part, other, direction, step):
        part = (part if other is None else part + other.astype(F32)).astype(BF)
        if direction > 0:
            return shift(part, "dp", [(i, i + 2) for i in range(2 * step)])
        return shift(part, "dp", [(i, i - 2) for i in range(8 - 2 * step, 8)])

    first = total(0, swapped(0))
    moved = lax.optimization_barrier((swapped(1), send(first, None, 1, 1), send(first, None, -1, 1)))
    second = total(1, moved[0])
    up = send(jnp.where(z == 0, second, first), moved[1], 1, 2)
    down = send(jnp.where(z == 3, second, first), moved[2], -1, 2)
    moved = lax.optimization_barrier((swapped(2), up, down))
    third = total(2, moved[0])
    up = send(jnp.where(z == 1, second, third), moved[1], 1, 3)
    down = send(jnp.where(z == 2, second, third), moved[2], -1, 3)
    moved = lax.optimization_barrier((swapped(3), up, down))
    return (total(3, moved[0]) + moved[1].astype(F32) + moved[2].astype(F32)).astype(BF)


UNIT_ATTENTION = ((0, 0), (0, 1), (1, 2))
UNIT_FEED = ((1, 0), (1, 3))


def rows_of(ref):
    return ref[...].reshape(-1, ref.shape[-1])


def unit_spec(unit, blocks, like):
    return pl.BlockSpec((blocks,) + like.shape[1:], lambda *i: (unit, 0, 0))


def whole(like):
    rank = len(like.shape)
    return pl.BlockSpec(like.shape, lambda *i: (0,) * rank)


def tall(like, size):
    return pl.BlockSpec((size, like.shape[1]), lambda i: (i, 0))


def call(kernel, grid, ins, in_specs, outs, out_specs, flops, limit, scratch=(), name=None):
    moved = sum(math.prod(v.shape) * v.dtype.itemsize for v in list(ins) + list(outs))
    return pl.pallas_call(
        kernel,
        grid=grid,
        in_specs=in_specs,
        out_specs=out_specs,
        out_shape=outs,
        scratch_shapes=list(scratch),
        compiler_params=pltpu.CompilerParams(vmem_limit_bytes=limit << 20),
        cost_estimate=pl.CostEstimate(flops=int(flops), bytes_accessed=int(moved), transcendentals=0),
        name=name,
    )(*ins)


def row_block(count):
    return count // 2 if count % 32 == 0 else count


def pair_of(mine_ref, away_ref, group, value):
    wide = mine_ref.shape[2] // 2
    at = value * wide
    return jnp.concatenate([mine_ref[group, :, at : at + wide], away_ref[1 - group, :, at : at + wide]], axis=0)


def attend_kernel(
    size, causal, rows_ref, pair_ref, away_ref, own_ref, other_ref, mask_ref, place_ref,
    part_ref, e_ref, inverse_ref, mixed_ref, q_ref,
):
    wide = q_ref.shape[1] // 2
    heads = wide // size
    rows = rows_ref[...]
    count = rows.shape[0]
    lanes = lax.broadcasted_iota(jnp.int32, (count, wide), 1)
    if causal:
        allowed = place_ref[...] < mask_ref[...]
    else:
        one = (lanes == 0).astype(BF)
    ones = jnp.ones((pair_ref.shape[1] * 2, wide), BF)
    inverses = jnp.zeros((count, wide), F32)
    part = None
    for group, w_ref in enumerate((own_ref, other_ref)):
        weight = rows_of(w_ref)
        query = mm(rows, weight[:wide], NT).astype(BF)
        q_ref[:, group * wide : group * wide + wide] = query
        query = query.astype(F32) * size ** (-0.5)
        key = pair_of(pair_ref, away_ref, group, 0)
        if not causal:
            key = jnp.concatenate([key, mask_ref[...]], axis=1)
        value = jnp.concatenate([pair_of(pair_ref, away_ref, group, 1), ones], axis=1)
        mixed = None
        for h in range(heads):
            here = (lanes >= h * size) & (lanes < h * size + size)
            lhs = jnp.where(here, query, 0.0).astype(BF)
            if causal:
                scores = jnp.where(allowed, mm(lhs, key, NT), -1e30)
            else:
                scores = mm(jnp.concatenate([lhs, one], axis=1), key, NT)
            powers = jnp.exp(scores - jnp.max(scores, axis=1, keepdims=True)).astype(BF)
            e_ref[group * heads + h] = powers
            got = mm(powers, value, NN)
            inverse = 1.0 / got[:, wide:]
            inverses = jnp.where(lanes == group * heads + h, inverse, inverses)
            got = got[:, :wide] * inverse
            mixed = got if h == 0 else jnp.where(here, got, mixed)
        mixed = mixed.astype(BF)
        mixed_ref[:, group * wide : group * wide + wide] = mixed
        term = mm(mixed, weight[3 * wide :], NN)
        part = term if part is None else part + term
    inverse_ref[...] = inverses
    part_ref[...] = part.astype(BF)


def attend(rows, pair, away, weights, unit, causal, mask, place, size):
    own, other, blocks = weights
    count, width = rows.shape
    wide = pair.shape[2] // 2
    step = row_block(count)
    heads = 2 * wide // size
    spec = unit_spec(unit, blocks, own)
    sd = jax.ShapeDtypeStruct
    return call(
        functools.partial(attend_kernel, size, causal),
        (count // step,),
        [rows, pair, away, own, other, mask, place],
        [tall(rows, step), whole(pair), whole(away), spec, spec, tall(mask, step) if causal else whole(mask), whole(place)],
        [
            sd((count, width), BF), pltpu.HBM((heads, count, 2 * count), BF), sd((count, wide), F32),
            sd((count, 2 * wide), BF), sd((count, 2 * wide), BF),
        ],
        [
            pl.BlockSpec((step, width), lambda i: (i, 0)),
            pl.BlockSpec((heads, step, 2 * count), lambda i: (0, i, 0)),
            pl.BlockSpec((step, wide), lambda i: (i, 0)),
            pl.BlockSpec((step, 2 * wide), lambda i: (i, 0)),
            pl.BlockSpec((step, 2 * wide), lambda i: (i, 0)),
        ],
        16 * heads * count * count * size,
        32,
        name="attend",
    )


def attend_back_kernel(
    size, g_ref, e_ref, inverse_ref, mixed_ref, q_ref, pair_ref, away_ref, own_ref, other_ref,
    dq_ref, rows_ref, mine_ref, give_ref, total,
):
    step = pl.program_id(0)
    wide = q_ref.shape[1] // 2
    heads = wide // size
    count = pair_ref.shape[1]
    scale = size ** (-0.5)
    lanes = lax.broadcasted_iota(jnp.int32, (q_ref.shape[0], wide), 1)
    grad = g_ref[...]

    @pl.when(step == 0)
    def _():
        total[...] = jnp.zeros_like(total)

    rows = None
    for group, w_ref in enumerate((own_ref, other_ref)):
        weight = rows_of(w_ref)
        cols = slice(group * wide, group * wide + wide)
        key = pair_of(pair_ref, away_ref, group, 0)
        value = pair_of(pair_ref, away_ref, group, 1)
        back = mm(grad, weight[3 * wide :], NT).astype(BF).astype(F32)
        inner = back * mixed_ref[:, cols].astype(F32)
        inverses = [inverse_ref[:, group * heads + h : group * heads + h + 1] for h in range(heads)]
        spread = jnp.broadcast_to(inverses[0], back.shape)
        for h in range(1, heads):
            spread = jnp.where(lanes >= h * size, inverses[h], spread)
        back = back * spread
        inner = inner * spread
        back_t = back.T.astype(BF)
        query_t = (q_ref[:, cols].astype(F32) * scale).T.astype(BF)
        dq = None
        for h in range(heads):
            here = (lanes >= h * size) & (lanes < h * size + size)
            powers = e_ref[group * heads + h]
            level = jnp.sum(jnp.where(here, inner, 0.0), axis=1, keepdims=True)
            slope = mm(jnp.where(here, back, 0.0).astype(BF), value, NT)
            ds = (powers.astype(F32) * (slope - level)).astype(BF)
            got = mm(ds, key, NN)
            dq = got if h == 0 else jnp.where(here, got, dq)
            k_at = group * 2 * wide + h * size
            v_at = k_at + wide
            total[k_at : k_at + size, :] += mm(query_t[h * size : h * size + size], ds, NN)
            total[v_at : v_at + size, :] += mm(back_t[h * size : h * size + size], powers, NN)
        dq = (dq * scale).astype(BF)
        dq_ref[:, cols] = dq
        term = mm(dq, weight[:wide], NN)
        rows = term if rows is None else rows + term
    rows_ref[...] = rows.astype(rows_ref.dtype)

    @pl.when(step == pl.num_programs(0) - 1)
    def _():
        mine_ref[...] = total[:, :count]
        give_ref[: 2 * wide, :] = total[2 * wide :, count:].astype(BF)
        give_ref[2 * wide :, :] = total[: 2 * wide, count:].astype(BF)


def attend_back(grad, powers, inverse, mixed, query, pair, away, weights, unit, size, kind):
    own, other, blocks = weights
    count, width = grad.shape
    wide = inverse.shape[1]
    step = row_block(count)
    heads = 2 * wide // size
    spec = unit_spec(unit, blocks, own)
    sd = jax.ShapeDtypeStruct
    flat = sd((4 * wide, count), F32)
    return call(
        functools.partial(attend_back_kernel, size),
        (count // step,),
        [grad, powers, inverse, mixed, query, pair, away, own, other],
        [
            tall(grad, step), pl.BlockSpec((heads, step, 2 * count), lambda i: (0, i, 0)), tall(inverse, step),
            tall(mixed, step), tall(query, step), whole(pair), whole(away), spec, spec,
        ],
        [sd((count, 2 * wide), BF), sd((count, width), kind), flat, sd(flat.shape, BF)],
        [
            pl.BlockSpec((step, 2 * wide), lambda i: (i, 0)),
            pl.BlockSpec((step, width), lambda i: (i, 0)),
            whole(flat),
            whole(flat),
        ],
        32 * heads * count * count * size,
        32,
        scratch=[pltpu.VMEM((4 * wide, 2 * count), F32)],
        name="attend_back",
    )


def feed_kernel(rows_ref, own_in, other_in, own_out, other_out, part_ref, active_ref, slope_ref):
    rows = rows_ref[...]
    size = active_ref.shape[1] // 2
    part = None
    for group, (w_in, w_out) in enumerate(((own_in, own_out), (other_in, other_out))):
        u = mm(rows, rows_of(w_in), NT)
        phi = 0.5 + 0.5 * lax.erf(u * 0.5**0.5)
        active = (u * phi).astype(BF)
        active_ref[:, group * size : group * size + size] = active
        slope_ref[:, group * size : group * size + size] = (
            phi + u * (jnp.exp(-0.5 * u * u) * 0.3989422804014327)
        ).astype(BF)
        term = mm(active, rows_of(w_out), NN)
        part = term if part is None else part + term
    part_ref[...] = part.astype(BF)


def feed(rows, weights, unit):
    own, other, blocks = weights
    count, width = rows.shape
    step = row_block(count)
    size = 2 * blocks * own.shape[1]
    first, second = unit_spec(unit, blocks, own), unit_spec(unit + 1, blocks, own)
    sd = jax.ShapeDtypeStruct
    return call(
        feed_kernel, (count // step,), [rows, own, other, own, other], [tall(rows, step), first, first, second, second],
        [sd((count, width), BF), sd((count, size), BF), sd((count, size), BF)],
        [pl.BlockSpec((step, w), lambda i: (i, 0)) for w in (width, size, size)],
        4 * count * width * size,
        20,
        name="feed",
    )


def per_device(
    source,
    target,
    out_grad,
    src_len,
    tgt_len,
    owners,
    master,
    rotated_first_moment,
    rotated_second_moment,
    stat_left,
    stat_right,
    basis_left,
    basis_right,
    norm_params,
    norm_one,
    norm_two,
):
    tensor_count = lax.axis_size("tensor")
    me = lax.axis_index("tensor")
    core = me & 1
    head_count = HEADS // tensor_count
    col_count = FFB // tensor_count
    capacity = master.shape[1]
    slot_count = capacity * lax.axis_size("dp")
    row_count = source.shape[1]
    block_rows = master.shape[2]
    width = master.shape[3]

    half = max(capacity // 2, 1)
    sources, made = gather_owners(
        master[0].astype(BF),
        [
            lambda: (before(stat_right[0], basis_right[0], 0, half), gather_chips(source[0])),
            lambda: (before(stat_right[0], basis_right[0], half, capacity - half), gather_chips(target[0])),
            lambda: gather_chips(out_grad[0]),
        ],
    )
    (early, src), (late, tgt), cot = made
    slot_of = slot_positions(owners[0], capacity)
    which, row = owner_place(slot_of, capacity)
    order = [j for unit in (0, 3, 1, 2, 4, 5, 6) for j in range(unit * col_count, (unit + 1) * col_count)]
    order = jnp.array(order, jnp.int32)
    blocks = collect(sources, which[order], row[order], [2 * col_count, 5 * col_count])
    weights = [(part, swap_core(part), col_count) for part in blocks]
    wide = head_count * block_rows

    chips = tensor_count // 2
    local = lax.iota(jnp.int32, row_count * chips)
    own_pos = (local // row_count) * (2 * row_count) + core * row_count + local % row_count
    other_pos = own_pos + (1 - 2 * core) * row_count
    key_pos = jnp.concatenate([own_pos, other_pos])
    gains = norm_params[0]
    shifts = norm_params[1]
    src_size = src_len[0]
    tgt_size = tgt_len[0]
    total_rows = local.shape[0]
    place = key_pos[None, :]
    first_lane = lax.iota(jnp.int32, wide)[None, :] == 0
    enc_mask = jnp.where((key_pos[:, None] >= src_size) & first_lane, -1e30, 0.0).astype(BF)
    dec_mask = jnp.minimum(own_pos + 1, tgt_size)[:, None]
    keep_rows = (own_pos < tgt_size).astype(F32)[:, None]

    def matrices(place_of, start, stop):
        part, unit = place_of
        at = unit * col_count
        return [w[at + start : at + stop].reshape(-1, width) for w in weights[part][:2]]

    def attention(query_rows, key_rows, unit, causal):
        pair = jnp.stack([mm(key_rows, w, NT).astype(BF) for w in matrices(unit, head_count, 3 * head_count)])
        away = swap_core(pair)
        mask = dec_mask if causal else enc_mask
        part, *saved = attend(query_rows, pair, away, weights[unit[0]], unit[1], causal, mask, place, block_rows)
        return part, saved + [pair, away]

    def halves(first, second):
        half = first.shape[1] // 2
        return mm(first[:, :half], second, TN), mm(first[:, half:], second, TN)

    def attention_back(grad, saved, query_rows, key_rows, unit, together):
        powers, inverse, mixed, query, pair, away = saved
        grad_b = grad.astype(BF)
        dq, query_part, mine, give = attend_back(
            grad_b, powers, inverse, mixed, query, pair, away, weights[unit[0]], unit[1], block_rows, F32 if together else BF
        )
        both = (mine + swap_core(give).astype(F32)).astype(BF)
        parts = [both[: 2 * wide], both[2 * wide :]]
        key_part = sum(mm(p, w, TN) for p, w in zip(parts, matrices(unit, head_count, 3 * head_count)))
        if together:
            key_part = key_part + query_part
        grad_q = halves(dq, query_rows)
        grad_o = halves(mixed, grad_b)
        grads = [[grad_q[at], mm(parts[at], key_rows, NN), grad_o[at]] for at in range(2)]
        return grads, query_part, key_part

    def feeding(rows, unit):
        part, active, slope = feed(rows, weights[unit[0]], unit[1])
        return part, (active, slope)

    def feeding_back(grad, saved, rows, unit):
        active, slope = saved
        grad_b = grad.astype(BF)
        half = active.shape[1] // 2
        grads, part = [], 0.0
        for at, w_in, w_out in zip(range(2), matrices(unit, 0, col_count), matrices((unit[0], unit[1] + 1), 0, col_count)):
            cols = slice(at * half, at * half + half)
            du = (mm(grad_b, w_out, NT) * slope[:, cols].astype(F32)).astype(BF)
            part = part + mm(du, w_in, NN)
            grads.append([mm(du, rows, TN), mm(active[:, cols], grad_b, TN)])
        return grads, part

    one, three, four = UNIT_ATTENTION
    two, five = UNIT_FEED
    branch_one, saved_one = attention(src, src, one, False)
    z_one = src.astype(F32) + sum_chips(branch_one)
    h_one, pull_one = jax.vjp(layer_norm, z_one, gains[0], shifts[0])
    h_one_b = h_one.astype(BF)
    branch_two, saved_two = feeding(h_one_b, two)
    z_two = h_one + sum_chips(branch_two)
    encoded, pull_two = jax.vjp(layer_norm, z_two, gains[1], shifts[1])
    encoded_b = encoded.astype(BF)
    branch_three, saved_three = attention(tgt, tgt, three, True)
    z_three = tgt.astype(F32) + sum_chips(branch_three)
    g_one, pull_three = jax.vjp(layer_norm, z_three, gains[2], shifts[2])
    g_one_b = g_one.astype(BF)
    branch_four, saved_four = attention(g_one_b, encoded_b, four, False)
    count = total_rows // 2
    chunks = [slice(0, count), slice(count, total_rows)]
    hold = lax.optimization_barrier
    got_four = [other_chips(branch_four[at]) for at in chunks]
    fours, rows_fives, saves, terms, got_fives = [], [], [], [], []
    for k, at in enumerate(chunks):
        if k:
            got_four[k], terms[0] = hold((got_four[k], terms[0]))
        total = branch_four[at].astype(F32) + got_four[k]
        g_two, pull = jax.vjp(layer_norm, g_one[at] + total, gains[3], shifts[3])
        g_two_b = g_two.astype(BF)
        branch_five, saved_five = feeding(g_two_b, five)
        fours.append((g_two, pull))
        rows_fives.append(g_two_b)
        saves.append(saved_five)
        terms.append(branch_five)
        got_fives.append(other_chips(branch_five))
    got_fives[0], terms[1] = hold((got_fives[0], terms[1]))
    normed, grads_five, parts_five, weights_fives, got_back = [], [], [], [], []
    gain_five, shift_five = 0.0, 0.0
    for k, at in enumerate(chunks):
        if k:
            got_fives[k], parts_five[0] = hold((got_fives[k], parts_five[0]))
        total = terms[k].astype(F32) + got_fives[k]
        values, pull = jax.vjp(layer_norm, fours[k][0] + total, gains[4], shifts[4])
        normed.append(values)
        grad, gain, shift = pull(cot[at].astype(F32) * keep_rows[at])
        gain_five, shift_five = gain_five + gain, shift_five + shift
        weights_term, part = feeding_back(grad, saves[k], rows_fives[k], five)
        part = part.astype(BF)
        grads_five.append(grad)
        parts_five.append(part)
        weights_fives.append(weights_term)
        got_back.append(other_chips(part))
    got_back[0], parts_five[1] = hold((got_back[0], parts_five[1]))
    decoded = own_rows((jnp.concatenate(normed, axis=0) * keep_rows).astype(BF))
    back_five = [part.astype(F32) + got for part, got in zip(parts_five, got_back)]
    weights_five = [[p + q for p, q in zip(x, y)] for x, y in zip(*weights_fives)]
    back_four = [fours[k][1](grads_five[k] + back_five[k]) for k in range(2)]
    grad_z_four = jnp.concatenate([item[0] for item in back_four], axis=0)
    gain_four, shift_four = (back_four[0][i] + back_four[1][i] for i in (1, 2))
    weights_four, query_four, key_four = attention_back(grad_z_four, saved_four, g_one_b, encoded_b, four, False)
    grad_encoded = sum_chips(key_four)
    query_four, weights_four = lax.optimization_barrier((query_four, weights_four))
    query_sum = sum_chips(query_four)
    grad_z_two, gain_two, shift_two = pull_two(grad_encoded)
    weights_two, rows_two = feeding_back(grad_z_two, saved_two, h_one_b, two)
    query_sum, rows_two = lax.optimization_barrier((query_sum, rows_two.astype(BF)))
    sum_two = sum_chips(rows_two)
    grad_z_three, gain_three, shift_three = pull_three(grad_z_four + query_sum)
    weights_three, _, rows_three = attention_back(grad_z_three, saved_three, tgt, tgt, three, True)
    sum_two, rows_three = lax.optimization_barrier((sum_two, rows_three))
    tgt_grad = own_rows(grad_z_three) + sum_chips_own(rows_three)
    grad_z_one, gain_one, shift_one = pull_one(grad_z_two + sum_two)
    weights_one, _, rows_one = attention_back(grad_z_one, saved_one, src, src, one, True)
    src_grad = own_rows(grad_z_one) + sum_chips_own(rows_one)

    def reduce_core(grads):
        mine, give = [jnp.concatenate(part, axis=0) for part in grads]
        total = mine + swap_core(give.astype(BF)).astype(F32)
        return total.astype(BF).reshape(-1, block_rows, width)

    layers = [reduce_core(item) for item in (weights_one, weights_two, weights_three, weights_four, weights_five)]
    norm_local = jnp.stack(
        [
            jnp.stack([gain_one, gain_two, gain_three, gain_four, gain_five]),
            jnp.stack([shift_one, shift_two, shift_three, shift_four, shift_five]),
        ]
    )
    held = slot_of[None, :] == jnp.arange(slot_count, dtype=jnp.int32)[:, None]
    block_of = jnp.sum(jnp.where(held, jnp.arange(slot_of.shape[0], dtype=jnp.int32)[None, :], 0), axis=1)
    block_of = jnp.where(jnp.any(held, axis=1), block_of, slot_of.shape[0])
    own_grad = sum_to_owner(layers, block_of, capacity)
    norm_grad = sum_everywhere(norm_local)
    results = after(
        own_grad,
        master[0],
        rotated_first_moment[0],
        rotated_second_moment[0],
        stat_left[0],
        basis_left[0],
        stat_right[0],
        basis_right[0],
        early,
        late,
    )
    norm_one_new = 0.9 * norm_one + 0.1 * norm_grad
    norm_two_new = 0.999 * norm_two + 0.001 * norm_grad * norm_grad
    norm_new = norm_params - rate_vector * (norm_one_new / FIX_ONE) / (jnp.sqrt(norm_two_new / FIX_TWO) + 1e-08)
    return (
        decoded[None],
        src_grad[None],
        tgt_grad[None],
        results[0][None],
        results[1][None],
        results[2][None],
        results[3][None],
        results[4][None],
        results[5][None],
        results[6][None],
        results[7][None],
        norm_new,
        norm_one_new,
        norm_two_new,
    )


def solution(mesh):
    in_specs = (
        P("dp", "tensor", None),
        P("dp", "tensor", None),
        P("dp", "tensor", None),
        P("dp"),
        P("dp"),
        P("tensor", None),
        P("tensor", "dp", None, None),
        P("tensor", "dp", None, None),
        P("tensor", "dp", None, None),
        P("tensor", "dp", None, None),
        P("tensor", "dp", None, None),
        P("tensor", "dp", None, None),
        P("tensor", "dp", None, None),
        P(),
        P(),
        P(),
    )
    out_specs = (
        P("dp", "tensor", None),
        P("dp", "tensor", None),
        P("dp", "tensor", None),
        P("tensor", "dp", None, None),
        P("tensor", "dp", None, None),
        P("tensor", "dp", None, None),
        P("tensor", "dp", None, None),
        P("tensor", "dp", None, None),
        P("tensor", "dp", None, None),
        P("tensor", "dp", None, None),
        P("tensor", "dp", None, None),
        P(),
        P(),
        P(),
    )
    return jax.shard_map(
        per_device, mesh=mesh, in_specs=in_specs, out_specs=out_specs, check_vma=False
    )
```
